512 devices in a mesh: rows: 128 (over z, y, core), cols: 4 (over x).
Axes of the slice: x: 4, y: 8, z: 8, core: 2. Of those that a mesh axis runs over, the one named last changes fastest.
Arguments:
- matrix: float32 [262144, 512], P('rows', 'cols'), may hold values from -140 to 140, as said below
- order: int32 [2, 256], replicated, may hold values from 0 to 255, each once within a row
Outputs:
- density: float32 [262144, 512], P('rows', 'cols')
- col_rms: float32 [512], P('cols')
The draws below stay inside these ranges and needn't reach their ends.
Inputs may be any that keep to these rules, and one draw needn't show every extreme that they name: Each row of order is a permutation of 0 .. 255. `matrix`: entries are real numbers of order one to some tens.
All inputs are finite; a program needn't handle non-finite values.
Results may differ from the reference program's by a relative error of at most 0.0003.
Values sent between devices are 32-bit elements; how exact they have to be, the bound alone decides.
No kernel may reach another device: no remote copies, remote signals or barrier semaphores. Data moves between devices by JAX's collectives and lax.ppermute only.
A program may use at most 64 MiB of HBM per device.

```python
import jax
import jax.numpy as jnp
from jax import lax

BLOCK = 128
ROUNDS = 16
STEPS = 2
ORDER = 256
ROWS = 262144
N = 512
N_COLS = 4


def draw_matrix(key, part):
    key = jax.random.fold_in(key, 11)
    key_rows, key_cols, key_base = jax.random.split(key, 3)
    row_index = jnp.arange(ROWS, dtype=jnp.float32)
    row_trend = (3.0 ** (row_index / ROWS - 0.5))[:, None]
    row_scale = jnp.exp(jax.random.uniform(key_rows, (ROWS, 1), jnp.float32, jnp.log(0.3), jnp.log(3.0)))
    col_scale = jnp.exp(jax.random.uniform(key_cols, (1, N), jnp.float32, jnp.log(0.3), jnp.log(3.0)))
    values = jnp.clip(jax.random.normal(key_base, (ROWS, N), jnp.float32), -6.0, 6.0)
    return (values * row_trend * row_scale * col_scale).astype(jnp.float32)


def setup_inputs(seed: int = 0) -> dict:
    arg_keys = jax.random.split(jax.random.key(seed), 3)
    matrix = draw_matrix(jax.random.fold_in(arg_keys[2], 71), 0)
    order = jax.vmap(lambda own: jax.random.permutation(own, ORDER))(jax.random.split(arg_keys[1], STEPS)).reshape((STEPS, ORDER)).astype(jnp.int32)
    return dict(matrix=matrix, order=order)


eps = 1e-06

def rotate_pairs(gram, order_row, round_count):
    order_size = gram.shape[0]
    half_size = order_size // 2
    last_slot = order_size - 1
    basis_start = jnp.eye(order_size, dtype=gram.dtype)

    def one_round(round_index, state_pair):
        turned, rotation_basis = state_pair
        round_now = jnp.asarray(round_index).astype(jnp.int32)
        slot_index = jnp.arange(half_size, dtype=jnp.int32)
        left_slot = jnp.where(slot_index == 0, last_slot, (round_now + slot_index) % last_slot).astype(jnp.int32)
        right_slot = ((round_now - slot_index) % last_slot).astype(jnp.int32)
        col_left = order_row[left_slot]
        col_right = order_row[right_slot]
        diag_left = turned[col_left, col_left]
        diag_right = turned[col_right, col_right]
        cross_term = turned[col_left, col_right]
        rot_angle = 0.5 * jnp.arctan2(2.0 * cross_term, diag_right - diag_left)
        cosine = jnp.cos(rot_angle)
        sine_part = jnp.sin(rot_angle)
        rows_left = turned[col_left]
        rows_right = turned[col_right]
        turned = turned.at[col_left].set(cosine[:, None] * rows_left - sine_part[:, None] * rows_right)
        turned = turned.at[col_right].set(sine_part[:, None] * rows_left + cosine[:, None] * rows_right)
        cols_left = turned[:, col_left]
        cols_right = turned[:, col_right]
        turned = turned.at[:, col_left].set(cols_left * cosine - cols_right * sine_part)
        turned = turned.at[:, col_right].set(cols_left * sine_part + cols_right * cosine)
        vec_left = rotation_basis[:, col_left]
        vec_right = rotation_basis[:, col_right]
        rotation_basis = rotation_basis.at[:, col_left].set(vec_left * cosine - vec_right * sine_part)
        rotation_basis = rotation_basis.at[:, col_right].set(vec_left * sine_part + vec_right * cosine)
        return (turned, rotation_basis)
    return lax.fori_loop(0, round_count, one_round, (gram, basis_start))

def reference(matrix, order):
    row_total = matrix.shape[0]
    block_count = N_COLS
    current = matrix
    for tourney_step, distance in enumerate((1, N_COLS // 2)):
        group_count = block_count // (2 * distance)
        reshaped = current.reshape(row_total, group_count, 2, distance, BLOCK)
        pair_stack = reshaped.transpose(1, 3, 0, 2, 4).reshape(group_count * distance, row_total, 2 * BLOCK)
        order_row = order[tourney_step]

        def solve_pair(joined):
            gram = jnp.dot(joined.T, joined, precision=lax.Precision.HIGHEST, preferred_element_type=jnp.float32)
            turned, rotation_basis = rotate_pairs(gram, order_row, ROUNDS)
            return jnp.dot(joined, rotation_basis, precision=lax.Precision.HIGHEST, preferred_element_type=jnp.float32)
        rotated = lax.map(solve_pair, pair_stack)
        current = rotated.reshape(group_count, distance, row_total, 2, BLOCK).transpose(2, 0, 3, 1, 4).reshape(row_total, block_count * BLOCK)
    density = current * current
    col_rms = jnp.sqrt(lax.optimization_barrier(jnp.sum(density, axis=0)) / row_total + eps)
    return (density, col_rms)
```

```python
import jax
import jax.numpy as jnp
from jax import lax
from jax.experimental import pallas as pl
from jax.experimental.pallas import tpu as pltpu
from jax.sharding import Mesh, PartitionSpec as P

ROUNDS = 16
EPS = 1e-06
HIGHEST = lax.Precision.HIGHEST
NN = (((1,), (0,)), ((), ()))
NT = (((1,), (1,)), ((), ()))
TN = (((0,), (0,)), ((), ()))
PAIRS = ((0, 0), (0, 1), (1, 1), (2, 2), (2, 3), (3, 3), (0, 2), (0, 3), (1, 2), (1, 3))


def dot(a, b, dims=NN):
    return lax.dot_general(a, b, dims, precision=HIGHEST, preferred_element_type=jnp.float32)


def slot_at(place, turn):
    side, inner = place // 128, place % 128
    k = 16 * (inner % 8) + inner // 8
    moved = jnp.where(side == 0, turn + k, turn + 255 - k)
    moved = jnp.where(moved >= 255, moved - 255, moved)
    return jnp.where((side == 0) & (k == 0), 255, moved)


def place_by_column(order_row, turn, transposed):
    rows = lax.broadcasted_iota(jnp.int32, (256, 256), 0)
    cols = lax.broadcasted_iota(jnp.int32, (256, 256), 1)
    column_slot = (rows == order_row).astype(jnp.float32)
    place_slot = (slot_at(rows, turn) == cols).astype(jnp.float32)
    pair = (column_slot, place_slot) if transposed else (place_slot, column_slot)
    return lax.dot_general(*pair, NT, preferred_element_type=jnp.float32)


def rotation(cross, low, high):
    x = high - low
    y = cross + cross
    ax, ay = jnp.abs(x), jnp.abs(y)
    m = jnp.maximum(ax, ay)
    rm = 1.0 / jnp.maximum(m, 1e-37)
    xs = jnp.where(m > 0.0, ax * rm, 1.0)
    ys = y * rm
    r = lax.rsqrt(xs * xs + ys * ys)
    u = 0.5 + 0.5 * (xs * r)
    ru = lax.rsqrt(u)
    big = u * ru
    small = (0.5 * (ys * r)) * ru
    gap = cross * (small * ru)
    back = x < 0.0
    cs = jnp.where(back, jnp.abs(small), big)
    sn = jnp.where(back, jnp.where(y < 0.0, -big, big), small)
    return cs, sn, jnp.minimum(low, high) - gap, jnp.maximum(low, high) + gap


def one_round(src, dst, dsrc, ddst, cbuf, sbuf):
    row8 = lax.broadcasted_iota(jnp.int32, (8, 128), 0)
    first, last = row8 == 0, row8 == 7

    def put(buf, lead, new):
        top, bottom = new
        for t in range(15):
            tile = top[t + 1] if t else jnp.where(first, top[0], top[1])
            buf[(*lead[0], pl.ds(8 * t, 8))] = tile
            buf[(*lead[1], pl.ds(8 * t + 8, 8))] = bottom[t]
        buf[(*lead[0], pl.ds(120, 8))] = jnp.where(last, bottom[15], pltpu.roll(top[0], 7, 0))
        buf[(*lead[1], pl.ds(0, 8))] = jnp.where(first, top[1], pltpu.roll(bottom[15], 1, 0))

    for a in range(2):
        top, bottom = [], []
        for t in range(16):
            rows = pl.ds(8 * t, 8)
            part = src[a, 0, 0, rows] * src[a, 1, 2, rows] + src[a, 0, 1, rows] * src[a, 1, 3, rows]
            cross = jnp.broadcast_to(jnp.sum(part, axis=1, keepdims=True), (8, 128))
            cs, sn, low, high = rotation(cross, dsrc[a, 0, rows], dsrc[a, 1, rows])
            cbuf[a, rows] = cs
            sbuf[a, rows] = sn
            top.append(low)
            bottom.append(high)
        put(ddst, ((a, 0), (a, 1)), (top, bottom))
    for a in range(2):
        for lane in range(4):
            top, bottom = [], []
            for t in range(16):
                rows = pl.ds(8 * t, 8)
                cs, sn = cbuf[a, rows], sbuf[a, rows]
                p, q = src[a, 0, lane, rows], src[a, 1, lane, rows]
                top.append(cs * p - sn * q)
                bottom.append(sn * p + cs * q)
            put(dst, ((a, 0, lane), (a, 1, lane)), (top, bottom))


def rotate_kernel(g_ref, order_ref, qt_ref, rms_ref, xa, xb, da, db, cbuf, sbuf):
    total_rows = 262144.0

    def solve(grams, order_row):
        start = place_by_column(order_row, 0, False)
        for a in range(2):
            held = dot(start, grams[a])
            both = start * held
            diag = jnp.broadcast_to(jnp.sum(both, axis=1, keepdims=True), (256, 128))
            for side in range(2):
                rows = slice(128 * side, 128 * side + 128)
                da[a, side] = diag[rows]
                for lane in range(2):
                    cols = slice(128 * lane, 128 * lane + 128)
                    xa[a, side, lane] = start[rows, cols]
                    xa[a, side, lane + 2] = held[rows, cols]

        def two_rounds(_, carry):
            one_round(xa, xb, da, db, cbuf, sbuf)
            one_round(xb, xa, db, da, cbuf, sbuf)
            return carry

        lax.fori_loop(0, ROUNDS // 2, two_rounds, 0)
        end = place_by_column(order_row, ROUNDS, True)
        basis, held, diag = [], [], []
        for a in range(2):
            sides = [
                jnp.concatenate([jnp.concatenate([xa[a, side, lane] for side in range(2)], axis=0) for lane in range(4)], axis=1)
            ][0]
            back = dot(end, sides)
            basis.append(back[:, :256])
            held.append(back[:, 256:])
            place_diag = jnp.concatenate([da[a, 0], da[a, 1]], axis=0)
            diag.append(dot(place_diag[:, :8], end, (((0,), (1,)), ((), ()))))
        return basis, held, diag

    def square(i, j, k):
        b = g_ref[j]
        return jnp.concatenate(
            [jnp.concatenate([g_ref[i], b], axis=1), jnp.concatenate([b.T, g_ref[k]], axis=1)], axis=0
        )

    basis, held, _ = solve([square(0, 1, 2), square(3, 4, 5)], order_ref[0:1, :])
    turned = [dot(basis[a], held[a], NT) for a in range(2)]
    between = jnp.concatenate(
        [jnp.concatenate([g_ref[6], g_ref[7]], axis=1), jnp.concatenate([g_ref[8], g_ref[9]], axis=1)], axis=0
    )
    cross = dot(dot(basis[0], between), basis[1], NT)
    grams = []
    for a in range(2):
        half = slice(128 * a, 128 * a + 128)
        b = cross[half, half]
        grams.append(
            jnp.concatenate(
                [
                    jnp.concatenate([turned[0][half, half], b], axis=1),
                    jnp.concatenate([b.T, turned[1][half, half]], axis=1),
                ],
                axis=0,
            )
        )
    basis1, _, diag = solve(grams, order_ref[1:2, :])
    for a in range(2):
        half = slice(128 * a, 128 * a + 128)
        qt_ref[a, :, :256] = dot(basis1[a][:, :128], basis[0][half, :])
        qt_ref[a, :, 256:] = dot(basis1[a][:, 128:], basis[1][half, :])
        rms = jnp.sqrt(jnp.maximum(diag[a], 0.0) / total_rows + EPS)
        rms_ref[a] = rms[:, :128]
        rms_ref[a + 2] = rms[:, 128:]


def rotate(g, order):
    return pl.pallas_call(
        rotate_kernel,
        out_shape=(
            jax.ShapeDtypeStruct((2, 256, 512), jnp.float32),
            jax.ShapeDtypeStruct((4, 8, 128), jnp.float32),
        ),
        in_specs=[pl.BlockSpec(memory_space=pltpu.VMEM)] * 2,
        out_specs=[pl.BlockSpec(memory_space=pltpu.VMEM)] * 2,
        scratch_shapes=[
            pltpu.VMEM((2, 2, 4, 128, 128), jnp.float32),
            pltpu.VMEM((2, 2, 4, 128, 128), jnp.float32),
            pltpu.VMEM((2, 2, 128, 128), jnp.float32),
            pltpu.VMEM((2, 2, 128, 128), jnp.float32),
            pltpu.VMEM((2, 128, 128), jnp.float32),
            pltpu.VMEM((2, 128, 128), jnp.float32),
        ],
        compiler_params=pltpu.CompilerParams(vmem_limit_bytes=48 * 1024 * 1024),
    )(g, order)


def gram_kernel(m_ref, g_ref):
    joined = [jnp.concatenate([m_ref[2 * a], m_ref[2 * a + 1]], axis=1) for a in range(2)]
    first = dot(joined[0], joined[0], TN)
    second = dot(joined[1], joined[1], TN)
    between = dot(joined[0], joined[1], TN)
    low, high = slice(0, 128), slice(128, 256)
    for i, whole in enumerate((first, second)):
        g_ref[3 * i] = whole[low, low]
        g_ref[3 * i + 1] = whole[low, high]
        g_ref[3 * i + 2] = whole[high, high]
    g_ref[6] = between[low, low]
    g_ref[7] = between[low, high]
    g_ref[8] = between[high, low]
    g_ref[9] = between[high, high]


def density_kernel(m_ref, qt_ref, out_ref):
    joined = jnp.concatenate([m_ref[c] for c in range(4)], axis=1)
    for a in range(2):
        turned = dot(joined, qt_ref[a], NT)
        squares = turned * turned
        out_ref[a] = squares[:, :128]
        out_ref[a + 2] = squares[:, 128:]


def in_vmem(kernel, out_shape, count):
    return pl.pallas_call(
        kernel,
        out_shape=jax.ShapeDtypeStruct(out_shape, jnp.float32),
        in_specs=[pl.BlockSpec(memory_space=pltpu.VMEM)] * count,
        out_specs=pl.BlockSpec(memory_space=pltpu.VMEM),
        compiler_params=pltpu.CompilerParams(vmem_limit_bytes=48 * 1024 * 1024),
    )


def exchange(parts, axis):
    return lax.all_to_all(parts, axis, 0, 0, tiled=True)


def sum_part(value, axis):
    count = lax.axis_size(axis)
    return exchange(value.reshape(count, value.shape[0] // count, 128), axis).sum(0)


def collect(value, axis):
    return exchange(jnp.broadcast_to(value[None], (lax.axis_size(axis), *value.shape)), axis)


def local(matrix, order):
    blocks = exchange(matrix.reshape(4, 512, 128), "x")
    gram = in_vmem(gram_kernel, (10, 128, 128), 1)(blocks).reshape(1280, 128)
    for axis in ("core", "x", "y"):
        gram = sum_part(gram, axis)
    gram = collect(gram, "z").sum(0)
    for axis in ("y", "x", "core"):
        gram = collect(gram, axis).reshape(-1, 128)
    turns, rms = rotate(gram.reshape(10, 128, 128), order)
    density = exchange(in_vmem(density_kernel, (4, 512, 128), 2)(blocks, turns), "x")
    own = lax.dynamic_index_in_dim(rms, lax.axis_index("x"), 0, keepdims=False)
    return density.reshape(2048, 128), own[0]


def solution(mesh):
    fine = Mesh(mesh.devices.reshape(8, 8, 2, 4), ("z", "y", "core", "x"))
    rows = ("z", "y", "core")
    return jax.shard_map(
        local,
        mesh=fine,
        in_specs=(P(rows, "x"), P()),
        out_specs=(P(rows, "x"), P("x")),
        check_vma=False,
    )
```

```python
import jax
import jax.numpy as jnp
from jax import lax
from jax.experimental import pallas as pl
from jax.experimental.pallas import tpu as pltpu
from jax.sharding import Mesh, PartitionSpec as P

ROUNDS = 16
ROWS = 262144
EPS = 1e-06
HIGHEST = lax.Precision.HIGHEST
NN = (((1,), (0,)), ((), ()))
NT = (((1,), (1,)), ((), ()))
TN = (((0,), (0,)), ((), ()))
PAIRS = ((0, 0), (0, 1), (1, 1), (2, 2), (2, 3), (3, 3), (0, 2), (0, 3), (1, 2), (1, 3))
LIMIT = pltpu.CompilerParams(vmem_limit_bytes=48 * 1024 * 1024)
VMEM = pl.BlockSpec(memory_space=pltpu.VMEM)


def dot(a, b, dims=NN):
    return lax.dot_general(a, b, dims, precision=HIGHEST, preferred_element_type=jnp.float32)


def short_dot(a, b, dims=NN):
    return lax.dot_general(a, b, dims, preferred_element_type=jnp.float32)


def split(value, count):
    parts = []
    for _ in range(count):
        part = value.astype(jnp.bfloat16)
        value = value - part.astype(jnp.float32)
        parts.append(part)
    return parts


def pick(onehot, value, dims=NN):
    high, mid, low = (short_dot(onehot, part, dims) for part in split(value, 3))
    return high + (mid + low)


def slot_at(place, turn):
    side, inner = place // 128, place % 128
    k = 16 * (inner % 8) + inner // 8
    moved = jnp.where(side == 0, turn + k, turn + 255 - k)
    moved = jnp.where(moved >= 255, moved - 255, moved)
    return jnp.where((side == 0) & (k == 0), 255, moved)


def places_kernel(order_ref, start_ref, end_ref):
    rows = lax.broadcasted_iota(jnp.int32, (256, 256), 0)
    cols = lax.broadcasted_iota(jnp.int32, (256, 256), 1)
    first = (slot_at(rows, 0) == cols).astype(jnp.bfloat16)
    last = (slot_at(rows, ROUNDS) == cols).astype(jnp.bfloat16)
    for step in range(2):
        column_slot = (rows == order_ref[step : step + 1, :]).astype(jnp.bfloat16)
        start_ref[step] = short_dot(first, column_slot, NT).astype(jnp.bfloat16)
        end_ref[step] = short_dot(column_slot, last, NT).astype(jnp.bfloat16)


def rotation(cross, low, high):
    x = high - low
    y = cross + cross
    ax = jnp.abs(x)
    yy = y * y
    hh = x * x + yy + 1e-37
    h = hh * lax.rsqrt(hh)
    w = h + ax
    n = lax.rsqrt(w * w + yy)
    big = w * n
    small = y * n
    gap = h * small * small
    back = x < 0.0
    cs = jnp.where(back, small, big)
    sn = jnp.where(back, big, small)
    return cs, sn, jnp.minimum(low, high) - gap, jnp.maximum(low, high) + gap


def one_round(count, src, dst, dsrc, ddst, cbuf, sbuf):
    row8 = lax.broadcasted_iota(jnp.int32, (8, 128), 0)
    first, last = row8 == 0, row8 == 7

    def put(buf, lead, new):
        top, bottom = new
        for t in range(15):
            tile = top[t + 1] if t else jnp.where(first, top[0], top[1])
            buf[(*lead[0], pl.ds(8 * t, 8))] = tile
            buf[(*lead[1], pl.ds(8 * t + 8, 8))] = bottom[t]
        buf[(*lead[0], pl.ds(120, 8))] = jnp.where(last, bottom[15], pltpu.roll(top[0], 7, 0))
        buf[(*lead[1], pl.ds(0, 8))] = jnp.where(first, top[1], pltpu.roll(bottom[15], 1, 0))

    for a in range(count):
        top, bottom = [], []
        for t in range(16):
            rows = pl.ds(8 * t, 8)
            part = src[a, 0, 0, rows] * src[a, 1, 2, rows] + src[a, 0, 1, rows] * src[a, 1, 3, rows]
            cross = jnp.broadcast_to(jnp.sum(part, axis=1, keepdims=True), (8, 128))
            cs, sn, low, high = rotation(cross, dsrc[a, 0, rows], dsrc[a, 1, rows])
            cbuf[a, rows] = cs
            sbuf[a, rows] = sn
            top.append(low)
            bottom.append(high)
        put(ddst, ((a, 0), (a, 1)), (top, bottom))
    for a in range(count):
        for lane in range(4):
            top, bottom = [], []
            for t in range(16):
                rows = pl.ds(8 * t, 8)
                cs, sn = cbuf[a, rows], sbuf[a, rows]
                p, q = src[a, 0, lane, rows], src[a, 1, lane, rows]
                top.append(cs * p - sn * q)
                bottom.append(sn * p + cs * q)
            put(dst, ((a, 0, lane), (a, 1, lane)), (top, bottom))


def rotate_kernel(x_ref, g_ref, start_ref, end_ref, q_ref, rms_ref, xa, xb, da, db, cbuf, sbuf):
    own_pair, own_side = x_ref[0] % 2, x_ref[0] // 2
    half = pl.ds(pl.multiple_of(128 * own_pair, 128), 128)

    def solve(grams, step):
        start = start_ref[step]
        start32 = start.astype(jnp.float32)
        for a, gram in enumerate(grams):
            held = pick(start, gram)
            diag = jnp.broadcast_to(jnp.sum(start32 * held, axis=1, keepdims=True), (256, 128))
            for side in range(2):
                rows = slice(128 * side, 128 * side + 128)
                da[a, side] = diag[rows]
                for lane in range(2):
                    cols = slice(128 * lane, 128 * lane + 128)
                    xa[a, side, lane] = start32[rows, cols]
                    xa[a, side, lane + 2] = held[rows, cols]

        def two_rounds(_, carry):
            one_round(len(grams), xa, xb, da, db, cbuf, sbuf)
            one_round(len(grams), xb, xa, db, da, cbuf, sbuf)
            return carry

        lax.fori_loop(0, ROUNDS // 2, two_rounds, 0)

    def placed(a, lanes):
        sides = [jnp.concatenate([xa[a, side, lane] for lane in lanes], axis=1) for side in range(2)]
        return jnp.concatenate(sides, axis=0)

    def square(a, b, d):
        return jnp.concatenate([jnp.concatenate([a, b], axis=1), jnp.concatenate([b.T, d], axis=1)], axis=0)

    solve([square(g_ref[i], g_ref[i + 1], g_ref[i + 2]) for i in (0, 3)], 0)
    end = end_ref[0, half, :]
    both = [pick(end, placed(a, range(4))) for a in range(2)]
    basis = [value[:, :256] for value in both]
    turned = [dot(value[:, :256], value[:, 256:], NT) for value in both]
    between = jnp.concatenate(
        [jnp.concatenate([g_ref[6], g_ref[7]], axis=1), jnp.concatenate([g_ref[8], g_ref[9]], axis=1)], axis=0
    )
    cross = dot(dot(basis[0], between), basis[1], NT)
    solve([square(turned[0], cross, turned[1])], 1)
    end = end_ref[1, pl.ds(pl.multiple_of(128 * own_side, 128), 128), :]
    last = pick(end, placed(0, range(2)))
    turns = jnp.concatenate([dot(last[:, :128], basis[0]), dot(last[:, 128:], basis[1])], axis=1)
    high, low = split(turns, 2)
    q_ref[:128] = high
    q_ref[128:] = low
    diag = jnp.concatenate([da[0, 0], da[0, 1]], axis=0)
    squares = sum(short_dot(part[:, :8], end, (((0,), (1,)), ((), ()))) for part in reversed(split(diag, 3)))
    rms_ref[...] = jnp.sqrt(jnp.maximum(squares, 0.0) / ROWS + EPS)


def rotate(x_index, gram, start, end):
    return pl.pallas_call(
        rotate_kernel,
        out_shape=(
            jax.ShapeDtypeStruct((256, 512), jnp.bfloat16),
            jax.ShapeDtypeStruct((8, 128), jnp.float32),
        ),
        in_specs=[pl.BlockSpec(memory_space=pltpu.SMEM), VMEM, VMEM, VMEM],
        out_specs=[VMEM, VMEM],
        scratch_shapes=[
            pltpu.VMEM((2, 2, 4, 128, 128), jnp.float32),
            pltpu.VMEM((2, 2, 4, 128, 128), jnp.float32),
            pltpu.VMEM((2, 2, 128, 128), jnp.float32),
            pltpu.VMEM((2, 2, 128, 128), jnp.float32),
            pltpu.VMEM((2, 128, 128), jnp.float32),
            pltpu.VMEM((2, 128, 128), jnp.float32),
        ],
        compiler_params=LIMIT,
    )(x_index, gram, start, end)


def places(order):
    return pl.pallas_call(
        places_kernel,
        out_shape=(jax.ShapeDtypeStruct((2, 256, 256), jnp.bfloat16),) * 2,
        in_specs=[VMEM],
        out_specs=[VMEM, VMEM],
        compiler_params=LIMIT,
    )(order)


def gram_kernel(m_ref, g_ref):
    joined = [jnp.concatenate([m_ref[2 * a], m_ref[2 * a + 1]], axis=1) for a in range(2)]
    low, high = slice(0, 128), slice(128, 256)
    for i in range(2):
        whole = dot(joined[i], joined[i], TN)
        g_ref[3 * i] = whole[low, low]
        g_ref[3 * i + 1] = whole[low, high]
        g_ref[3 * i + 2] = whole[high, high]
    between = dot(joined[0], joined[1], TN)
    g_ref[6] = between[low, low]
    g_ref[7] = between[low, high]
    g_ref[8] = between[high, low]
    g_ref[9] = between[high, high]


def grams(blocks):
    return pl.pallas_call(
        gram_kernel,
        out_shape=jax.ShapeDtypeStruct((10, 128, 128), jnp.float32),
        in_specs=[VMEM],
        out_specs=VMEM,
        compiler_params=LIMIT,
    )(blocks)


def density_kernel(m_ref, q_ref, out_ref):
    joined = jnp.concatenate([m_ref[c] for c in range(4)], axis=1)
    high, low = split(joined, 2)
    wide = short_dot(high, q_ref[...], NT)
    turned = wide[:, :128] + (wide[:, 128:] + short_dot(low, q_ref[:128, :], NT))
    out_ref[...] = turned * turned


def densities(whole, turns):
    rows = whole.shape[1]
    return pl.pallas_call(
        density_kernel,
        grid=(4,),
        out_shape=jax.ShapeDtypeStruct((rows, 128), jnp.float32),
        in_specs=[
            pl.BlockSpec((4, rows // 4, 128), lambda i: (0, i, 0)),
            pl.BlockSpec((256, 512), lambda i: (0, 0)),
        ],
        out_specs=pl.BlockSpec((rows // 4, 128), lambda i: (i, 0)),
        compiler_params=LIMIT,
    )(whole, turns)


def exchange(parts, axis):
    return lax.all_to_all(parts, axis, 0, 0, tiled=True)


def sum_part(value, axis):
    count = lax.axis_size(axis)
    return exchange(value.reshape(count, value.shape[0] // count, 128), axis).sum(0)


def collect(value, axis):
    return exchange(jnp.broadcast_to(value[None], (lax.axis_size(axis), *value.shape)), axis)


def local(matrix, order):
    start, end = places(order)
    blocks = exchange(matrix.reshape(4, 512, 128), "x")
    matrix, blocks = lax.optimization_barrier((matrix, blocks))
    whole = lax.all_gather(matrix, "x")
    gram = grams(blocks).reshape(1280, 128)
    for axis in ("core", "x", "y"):
        gram = sum_part(gram, axis)
    gram = collect(gram, "z").sum(0)
    for axis in ("y", "x", "core"):
        gram = collect(gram, axis).reshape(-1, 128)
    x_index = lax.axis_index("x").astype(jnp.int32).reshape(1)
    turns, rms = rotate(x_index, gram.reshape(10, 128, 128), start, end)
    return densities(whole, turns), rms[0]


def solution(mesh):
    fine = Mesh(mesh.devices.reshape(8, 8, 2, 4), ("z", "y", "core", "x"))
    rows = ("z", "y", "core")
    return jax.shard_map(
        local,
        mesh=fine,
        in_specs=(P(rows, "x"), P()),
        out_specs=(P(rows, "x"), P("x")),
        check_vma=False,
    )
```

```python
import jax
import jax.numpy as jnp
from jax import lax
from jax.experimental import pallas as pl
from jax.experimental.pallas import tpu as pltpu
from jax.sharding import Mesh, PartitionSpec as P

ROUNDS = 16
ROWS = 262144
EPS = 1e-06
HIGHEST = lax.Precision.HIGHEST
NN = (((1,), (0,)), ((), ()))
NT = (((1,), (1,)), ((), ()))
TN = (((0,), (0,)), ((), ()))
PAIRS = ((0, 0), (0, 1), (1, 1), (2, 2), (2, 3), (3, 3), (0, 2), (0, 3), (1, 2), (1, 3))
LIMIT = pltpu.CompilerParams(vmem_limit_bytes=48 * 1024 * 1024)
VMEM = pl.BlockSpec(memory_space=pltpu.VMEM)
SMEM = pl.BlockSpec(memory_space=pltpu.SMEM)
HBM = pl.BlockSpec(memory_space=pltpu.HBM)
CHUNKS = 4


def dot(a, b, dims=NN):
    return lax.dot_general(a, b, dims, precision=HIGHEST, preferred_element_type=jnp.float32)


def short_dot(a, b, dims=NN):
    return lax.dot_general(a, b, dims, preferred_element_type=jnp.float32)


def split(value, count):
    parts = []
    for _ in range(count):
        part = value.astype(jnp.bfloat16)
        value = value - part.astype(jnp.float32)
        parts.append(part)
    return parts


def pick(onehot, value, dims=NN):
    high, mid, low = (short_dot(onehot, part, dims) for part in split(value, 3))
    return high + (mid + low)


def slot_at(place, turn):
    side, inner = place // 128, place % 128
    k = 16 * (inner % 8) + inner // 8
    moved = jnp.where(side == 0, turn + k, turn + 255 - k)
    moved = jnp.where(moved >= 255, moved - 255, moved)
    return jnp.where((side == 0) & (k == 0), 255, moved)


def places_kernel(order_ref, start_ref, end_ref):
    rows = lax.broadcasted_iota(jnp.int32, (256, 256), 0)
    cols = lax.broadcasted_iota(jnp.int32, (256, 256), 1)
    first = (slot_at(rows, 0) == cols).astype(jnp.bfloat16)
    last = (slot_at(rows, ROUNDS) == cols).astype(jnp.bfloat16)
    for step in range(2):
        column_slot = (rows == order_ref[step : step + 1, :]).astype(jnp.bfloat16)
        start_ref[step] = short_dot(first, column_slot, NT).astype(jnp.bfloat16)
        end_ref[step] = short_dot(column_slot, last, NT).astype(jnp.bfloat16)


def rotation(cross, low, high):
    x = high - low
    y = cross + cross
    ax = jnp.abs(x)
    yy = y * y
    hh = x * x + yy + 1e-37
    h = hh * lax.rsqrt(hh)
    w = h + ax
    n = lax.rsqrt(w * w + yy)
    big = w * n
    small = y * n
    gap = h * small * small
    back = x < 0.0
    cs = jnp.where(back, small, big)
    sn = jnp.where(back, big, small)
    return cs, sn, jnp.minimum(low, high) - gap, jnp.maximum(low, high) + gap


def one_round(count, src, dst, dsrc, ddst, cbuf, sbuf):
    row8 = lax.broadcasted_iota(jnp.int32, (8, 128), 0)
    first, last = row8 == 0, row8 == 7

    def put(buf, lead, new):
        top, bottom = new
        for t in range(15):
            tile = top[t + 1] if t else jnp.where(first, top[0], top[1])
            buf[(*lead[0], pl.ds(8 * t, 8))] = tile
            buf[(*lead[1], pl.ds(8 * t + 8, 8))] = bottom[t]
        buf[(*lead[0], pl.ds(120, 8))] = jnp.where(last, bottom[15], pltpu.roll(top[0], 7, 0))
        buf[(*lead[1], pl.ds(0, 8))] = jnp.where(first, top[1], pltpu.roll(bottom[15], 1, 0))

    for a in range(count):
        top, bottom = [], []
        for t in range(16):
            rows = pl.ds(8 * t, 8)
            part = src[a, 0, 0, rows] * src[a, 1, 2, rows] + src[a, 0, 1, rows] * src[a, 1, 3, rows]
            cross = jnp.broadcast_to(jnp.sum(part, axis=1, keepdims=True), (8, 128))
            cs, sn, low, high = rotation(cross, dsrc[a, 0, rows], dsrc[a, 1, rows])
            cbuf[a, rows] = cs
            sbuf[a, rows] = sn
            top.append(low)
            bottom.append(high)
        put(ddst, ((a, 0), (a, 1)), (top, bottom))
    for a in range(count):
        for lane in range(4):
            top, bottom = [], []
            for t in range(16):
                rows = pl.ds(8 * t, 8)
                cs, sn = cbuf[a, rows], sbuf[a, rows]
                p, q = src[a, 0, lane, rows], src[a, 1, lane, rows]
                top.append(cs * p - sn * q)
                bottom.append(sn * p + cs * q)
            put(dst, ((a, 0, lane), (a, 1, lane)), (top, bottom))


def rotate_kernel(
    place_ref, own_ref, other_ref, start_ref, end_ref, whole_ref, out_ref, rms_ref,
    g_ref, xa, xb, da, db, cbuf, sbuf, held_rows, squares, in_sems, out_sems,
):
    rows_each = held_rows.shape[2]
    fetch = []
    for i in range(CHUNKS):
        rows = pl.ds(i * rows_each, rows_each)
        fetch.append(pltpu.make_async_copy(whole_ref.at[:, rows, :], held_rows.at[i], in_sems.at[i]))
        fetch[-1].start()
    core = place_ref[1]
    g_ref[pl.ds(5 * core, 5)] = own_ref[...]
    g_ref[pl.ds(5 * (1 - core), 5)] = other_ref[...]
    own_pair, own_side = place_ref[0] % 2, place_ref[0] // 2
    half = pl.ds(pl.multiple_of(128 * own_pair, 128), 128)

    def solve(grams, step):
        start = start_ref[step]
        start32 = start.astype(jnp.float32)
        for a, gram in enumerate(grams):
            held = pick(start, gram)
            diag = jnp.broadcast_to(jnp.sum(start32 * held, axis=1, keepdims=True), (256, 128))
            for side in range(2):
                rows = slice(128 * side, 128 * side + 128)
                da[a, side] = diag[rows]
                for lane in range(2):
                    cols = slice(128 * lane, 128 * lane + 128)
                    xa[a, side, lane] = start32[rows, cols]
                    xa[a, side, lane + 2] = held[rows, cols]

        def two_rounds(_, carry):
            one_round(len(grams), xa, xb, da, db, cbuf, sbuf)
            one_round(len(grams), xb, xa, db, da, cbuf, sbuf)
            return carry

        lax.fori_loop(0, ROUNDS // 2, two_rounds, 0)

    def placed(a, lanes):
        sides = [jnp.concatenate([xa[a, side, lane] for lane in lanes], axis=1) for side in range(2)]
        return jnp.concatenate(sides, axis=0)

    def square(a, b, d):
        return jnp.concatenate([jnp.concatenate([a, b], axis=1), jnp.concatenate([b.T, d], axis=1)], axis=0)

    solve([square(g_ref[i], g_ref[i + 1], g_ref[i + 2]) for i in (0, 3)], 0)
    end = end_ref[0, half, :]
    both = [pick(end, placed(a, range(4))) for a in range(2)]
    basis = [value[:, :256] for value in both]
    turned = [dot(value[:, :256], value[:, 256:], NT) for value in both]
    between = jnp.concatenate(
        [jnp.concatenate([g_ref[6], g_ref[7]], axis=1), jnp.concatenate([g_ref[8], g_ref[9]], axis=1)], axis=0
    )
    cross = dot(dot(basis[0], between), basis[1], NT)
    solve([square(turned[0], cross, turned[1])], 1)
    end = end_ref[1, pl.ds(pl.multiple_of(128 * own_side, 128), 128), :]
    last = pick(end, placed(0, range(2)))
    turns = jnp.concatenate([dot(last[:, :128], basis[0]), dot(last[:, 128:], basis[1])], axis=1)
    diag = jnp.concatenate([da[0, 0], da[0, 1]], axis=0)
    sums = sum(short_dot(part[:, :8], end, (((0,), (1,)), ((), ()))) for part in reversed(split(diag, 3)))
    rms_ref[...] = jnp.sqrt(jnp.maximum(sums[:1], 0.0) / ROWS + EPS)
    turn_high, turn_low = split(turns, 2)
    both = jnp.concatenate([turn_high, turn_low], axis=0)
    store = []
    for i in range(CHUNKS):
        fetch[i].wait()
        high, low = split(jnp.concatenate([held_rows[i, c] for c in range(4)], axis=1), 2)
        wide = short_dot(high, both, NT)
        value = wide[:, :128] + (wide[:, 128:] + short_dot(low, turn_high, NT))
        rows = pl.ds(i * rows_each, rows_each)
        squares[rows, :] = value * value
        store.append(pltpu.make_async_copy(squares.at[rows, :], out_ref.at[rows, :], out_sems.at[i]))
        store[-1].start()
    for copy in store:
        copy.wait()


def rotate(place, own, other, start, end, whole):
    rows = whole.shape[1]
    return pl.pallas_call(
        rotate_kernel,
        out_shape=(
            jax.ShapeDtypeStruct((rows, 128), jnp.float32),
            jax.ShapeDtypeStruct((1, 128), jnp.float32),
        ),
        in_specs=[SMEM, VMEM, VMEM, VMEM, VMEM, HBM],
        out_specs=[HBM, VMEM],
        scratch_shapes=[
            pltpu.VMEM((10, 128, 128), jnp.float32),
            pltpu.VMEM((2, 2, 4, 128, 128), jnp.float32),
            pltpu.VMEM((2, 2, 4, 128, 128), jnp.float32),
            pltpu.VMEM((2, 2, 128, 128), jnp.float32),
            pltpu.VMEM((2, 2, 128, 128), jnp.float32),
            pltpu.VMEM((2, 128, 128), jnp.float32),
            pltpu.VMEM((2, 128, 128), jnp.float32),
            pltpu.VMEM((CHUNKS, 4, rows // CHUNKS, 128), jnp.float32),
            pltpu.VMEM((rows, 128), jnp.float32),
            pltpu.SemaphoreType.DMA((CHUNKS,)),
            pltpu.SemaphoreType.DMA((CHUNKS,)),
        ],
        compiler_params=pltpu.CompilerParams(vmem_limit_bytes=52 * 1024 * 1024),
    )(place, own, other, start, end, whole)


def places(order):
    return pl.pallas_call(
        places_kernel,
        out_shape=(jax.ShapeDtypeStruct((2, 256, 256), jnp.bfloat16),) * 2,
        in_specs=[VMEM],
        out_specs=[VMEM, VMEM],
        compiler_params=LIMIT,
    )(order)


def gram_kernel(core_ref, m_ref, mine_ref, theirs_ref):
    parts = [split(jnp.concatenate([m_ref[2 * a], m_ref[2 * a + 1]], axis=1), 2) for a in range(2)]

    def product(left, right):
        (lh, ll), (rh, rl) = left, right
        small = (short_dot(lh, rl, TN) + short_dot(ll, rh, TN)) + short_dot(ll, rl, TN)
        return short_dot(lh, rh, TN) + small

    low, high = slice(0, 128), slice(128, 256)
    blocks = []
    for part in parts:
        whole = product(part, part)
        blocks += [whole[low, low], whole[low, high], whole[high, high]]
    between = product(*parts)
    blocks += [between[low, low], between[low, high], between[high, low], between[high, high]]
    for core, halves in enumerate(((mine_ref, theirs_ref), (theirs_ref, mine_ref))):

        @pl.when(core_ref[0] == core)
        def _(halves=halves):
            for i, block in enumerate(blocks):
                halves[i // 5][i % 5] = block


def grams(core_index, blocks):
    return pl.pallas_call(
        gram_kernel,
        out_shape=(jax.ShapeDtypeStruct((5, 128, 128), jnp.float32),) * 2,
        in_specs=[SMEM, VMEM],
        out_specs=[VMEM, VMEM],
        compiler_params=LIMIT,
    )(core_index, blocks)


def exchange(parts, axis):
    return lax.all_to_all(parts, axis, 0, 0, tiled=True)


def sum_part(value, axis):
    count = lax.axis_size(axis)
    return exchange(value.reshape(count, value.shape[0] // count, 128), axis).sum(0)


def collect(value, axis):
    return exchange(jnp.broadcast_to(value[None], (lax.axis_size(axis), *value.shape)), axis)


def swap_cores(value):
    return lax.ppermute(value, "core", ((0, 1), (1, 0)))


def local(matrix, order):
    place = jnp.stack([lax.axis_index("x"), lax.axis_index("core")]).astype(jnp.int32)
    start, end = places(order)
    blocks = exchange(matrix.reshape(4, 512, 128), "x")
    matrix, blocks = lax.optimization_barrier((matrix, blocks))
    whole = lax.all_gather(matrix, "x")
    mine, theirs = grams(place[1:], blocks)
    gram = (mine + swap_cores(theirs)).reshape(640, 128)
    for axis in ("x", "y"):
        gram = sum_part(gram, axis)
    gram = collect(gram, "z").sum(0)
    for axis in ("y", "x"):
        gram = collect(gram, axis).reshape(-1, 128)
    own = gram.reshape(5, 128, 128)
    density, rms = rotate(place, own, swap_cores(own), start, end, whole)
    return density, rms.reshape(128)


def solution(mesh):
    fine = Mesh(mesh.devices.reshape(8, 8, 2, 4), ("z", "y", "core", "x"))
    rows = ("z", "y", "core")
    return jax.shard_map(
        local,
        mesh=fine,
        in_specs=(P(rows, "x"), P()),
        out_specs=(P(rows, "x"), P("x")),
        check_vma=False,
    )
```

```python
import jax
import jax.numpy as jnp
from jax import lax
from jax.experimental import pallas as pl
from jax.experimental.pallas import tpu as pltpu
from jax.sharding import Mesh, PartitionSpec as P

ROUNDS = 16
ROWS = 262144
EPS = 1e-06
HIGHEST = lax.Precision.HIGHEST
NN = (((1,), (0,)), ((), ()))
NT = (((1,), (1,)), ((), ()))
TN = (((0,), (0,)), ((), ()))
PAIRS = ((0, 0), (0, 1), (1, 1), (2, 2), (2, 3), (3, 3), (0, 2), (0, 3), (1, 2), (1, 3))
LIMIT = pltpu.CompilerParams(vmem_limit_bytes=48 * 1024 * 1024)
VMEM = pl.BlockSpec(memory_space=pltpu.VMEM)
SMEM = pl.BlockSpec(memory_space=pltpu.SMEM)
HBM = pl.BlockSpec(memory_space=pltpu.HBM)
CHUNKS = 4


def dot(a, b, dims=NN):
    return lax.dot_general(a, b, dims, precision=HIGHEST, preferred_element_type=jnp.float32)


def short_dot(a, b, dims=NN):
    return lax.dot_general(a, b, dims, preferred_element_type=jnp.float32)


def split(value, count):
    parts = []
    for _ in range(count):
        part = value.astype(jnp.bfloat16)
        value = value - part.astype(jnp.float32)
        parts.append(part)
    return parts


def pick(onehot, value, dims=NN):
    high, mid, low = (short_dot(onehot, part, dims) for part in split(value, 3))
    return high + (mid + low)


def slot_at(place, turn):
    side, inner = place // 128, place % 128
    k = 16 * (inner % 8) + inner // 8
    moved = jnp.where(side == 0, turn + k, turn + 255 - k)
    moved = jnp.where(moved >= 255, moved - 255, moved)
    return jnp.where((side == 0) & (k == 0), 255, moved)


def places_kernel(order_ref, start_ref, end_ref):
    rows = lax.broadcasted_iota(jnp.int32, (256, 256), 0)
    cols = lax.broadcasted_iota(jnp.int32, (256, 256), 1)
    first = (slot_at(rows, 0) == cols).astype(jnp.bfloat16)
    last = (slot_at(rows, ROUNDS) == cols).astype(jnp.bfloat16)
    for step in range(2):
        column_slot = (rows == order_ref[step : step + 1, :]).astype(jnp.bfloat16)
        start_ref[step] = short_dot(first, column_slot, NT).astype(jnp.bfloat16)
        end_ref[step] = short_dot(column_slot, last, NT).astype(jnp.bfloat16)


def rotation(cross, low, high):
    x = high - low
    y = cross + cross
    ax = jnp.abs(x)
    yy = y * y
    hh = x * x + yy + 1e-37
    h = hh * lax.rsqrt(hh)
    w = h + ax
    n = lax.rsqrt(w * w + yy)
    big = w * n
    small = y * n
    gap = h * small * small
    back = x < 0.0
    cs = jnp.where(back, small, big)
    sn = jnp.where(back, big, small)
    return cs, sn, jnp.minimum(low, high) - gap, jnp.maximum(low, high) + gap


def one_round(count, src, dst, dsrc, ddst, cbuf, sbuf):
    row8 = lax.broadcasted_iota(jnp.int32, (8, 128), 0)
    first, last = row8 == 0, row8 == 7

    def put(buf, lead, new):
        top, bottom = new
        for t in range(15):
            tile = top[t + 1] if t else jnp.where(first, top[0], top[1])
            buf[(*lead[0], pl.ds(8 * t, 8))] = tile
            buf[(*lead[1], pl.ds(8 * t + 8, 8))] = bottom[t]
        buf[(*lead[0], pl.ds(120, 8))] = jnp.where(last, bottom[15], pltpu.roll(top[0], 7, 0))
        buf[(*lead[1], pl.ds(0, 8))] = jnp.where(first, top[1], pltpu.roll(bottom[15], 1, 0))

    for a in range(count):
        top, bottom = [], []
        for t in range(16):
            rows = pl.ds(8 * t, 8)
            part = src[a, 0, 0, rows] * src[a, 1, 2, rows] + src[a, 0, 1, rows] * src[a, 1, 3, rows]
            cross = jnp.broadcast_to(jnp.sum(part, axis=1, keepdims=True), (8, 128))
            cs, sn, low, high = rotation(cross, dsrc[a, 0, rows], dsrc[a, 1, rows])
            cbuf[a, rows] = cs
            sbuf[a, rows] = sn
            top.append(low)
            bottom.append(high)
        put(ddst, ((a, 0), (a, 1)), (top, bottom))
    for a in range(count):
        for lane in range(4):
            top, bottom = [], []
            for t in range(16):
                rows = pl.ds(8 * t, 8)
                cs, sn = cbuf[a, rows], sbuf[a, rows]
                p, q = src[a, 0, lane, rows], src[a, 1, lane, rows]
                top.append(cs * p - sn * q)
                bottom.append(sn * p + cs * q)
            put(dst, ((a, 0, lane), (a, 1, lane)), (top, bottom))


def rotate_kernel(
    place_ref, own_ref, other_ref, start_ref, end_ref, whole_ref, out_ref, rms_ref,
    g_ref, xa, xb, da, db, cbuf, sbuf, held_rows, squares, in_sems, out_sems,
):
    rows_each = held_rows.shape[2]
    fetch = []
    for i in range(CHUNKS):
        rows = pl.ds(i * rows_each, rows_each)
        fetch.append(pltpu.make_async_copy(whole_ref.at[:, rows, :], held_rows.at[i], in_sems.at[i]))
        fetch[-1].start()
    core = place_ref[1]
    g_ref[pl.ds(5 * core, 5)] = own_ref[...]
    g_ref[pl.ds(5 * (1 - core), 5)] = other_ref[...]
    own_pair, own_side = place_ref[0] % 2, place_ref[0] // 2
    half = pl.ds(pl.multiple_of(128 * own_pair, 128), 128)

    def solve(grams, step):
        start = start_ref[step]
        start32 = start.astype(jnp.float32)
        for a, gram in enumerate(grams):
            held = pick(start, gram)
            diag = jnp.broadcast_to(jnp.sum(start32 * held, axis=1, keepdims=True), (256, 128))
            for side in range(2):
                rows = slice(128 * side, 128 * side + 128)
                da[a, side] = diag[rows]
                for lane in range(2):
                    cols = slice(128 * lane, 128 * lane + 128)
                    xa[a, side, lane] = start32[rows, cols]
                    xa[a, side, lane + 2] = held[rows, cols]

        def two_rounds(_, carry):
            one_round(len(grams), xa, xb, da, db, cbuf, sbuf)
            one_round(len(grams), xb, xa, db, da, cbuf, sbuf)
            return carry

        lax.fori_loop(0, ROUNDS // 2, two_rounds, 0)

    def placed(a, lanes):
        sides = [jnp.concatenate([xa[a, side, lane] for lane in lanes], axis=1) for side in range(2)]
        return jnp.concatenate(sides, axis=0)

    def square(a, b, d):
        return jnp.concatenate([jnp.concatenate([a, b], axis=1), jnp.concatenate([b.T, d], axis=1)], axis=0)

    solve([square(g_ref[i], g_ref[i + 1], g_ref[i + 2]) for i in (0, 3)], 0)
    end = end_ref[0, half, :]
    both = [pick(end, placed(a, range(4))) for a in range(2)]
    basis = [value[:, :256] for value in both]
    turned = [dot(value[:, :256], value[:, 256:], NT) for value in both]
    between = jnp.concatenate(
        [jnp.concatenate([g_ref[6], g_ref[7]], axis=1), jnp.concatenate([g_ref[8], g_ref[9]], axis=1)], axis=0
    )
    cross = dot(dot(basis[0], between), basis[1], NT)
    solve([square(turned[0], cross, turned[1])], 1)
    end = end_ref[1, pl.ds(pl.multiple_of(128 * own_side, 128), 128), :]
    last = pick(end, placed(0, range(2)))
    turns = jnp.concatenate([dot(last[:, :128], basis[0]), dot(last[:, 128:], basis[1])], axis=1)
    diag = jnp.concatenate([da[0, 0], da[0, 1]], axis=0)
    sums = sum(short_dot(part[:, :8], end, (((0,), (1,)), ((), ()))) for part in reversed(split(diag, 3)))
    rms_ref[...] = jnp.sqrt(jnp.maximum(sums[:1], 0.0) / ROWS + EPS)
    turn_high, turn_low = split(turns, 2)
    both = jnp.concatenate([turn_high, turn_low], axis=0)
    store = []
    for i in range(CHUNKS):
        fetch[i].wait()
        high, low = split(jnp.concatenate([held_rows[i, c] for c in range(4)], axis=1), 2)
        wide = short_dot(high, both, NT)
        value = wide[:, :128] + (wide[:, 128:] + short_dot(low, turn_high, NT))
        rows = pl.ds(i * rows_each, rows_each)
        squares[rows, :] = value * value
        store.append(pltpu.make_async_copy(squares.at[rows, :], out_ref.at[rows, :], out_sems.at[i]))
        store[-1].start()
    for copy in store:
        copy.wait()


def rotate(place, own, other, start, end, whole):
    rows = whole.shape[1]
    return pl.pallas_call(
        rotate_kernel,
        out_shape=(
            jax.ShapeDtypeStruct((rows, 128), jnp.float32),
            jax.ShapeDtypeStruct((1, 128), jnp.float32),
        ),
        in_specs=[SMEM, VMEM, VMEM, VMEM, VMEM, HBM],
        out_specs=[HBM, VMEM],
        scratch_shapes=[
            pltpu.VMEM((10, 128, 128), jnp.float32),
            pltpu.VMEM((2, 2, 4, 128, 128), jnp.float32),
            pltpu.VMEM((2, 2, 4, 128, 128), jnp.float32),
            pltpu.VMEM((2, 2, 128, 128), jnp.float32),
            pltpu.VMEM((2, 2, 128, 128), jnp.float32),
            pltpu.VMEM((2, 128, 128), jnp.float32),
            pltpu.VMEM((2, 128, 128), jnp.float32),
            pltpu.VMEM((CHUNKS, 4, rows // CHUNKS, 128), jnp.float32),
            pltpu.VMEM((rows, 128), jnp.float32),
            pltpu.SemaphoreType.DMA((CHUNKS,)),
            pltpu.SemaphoreType.DMA((CHUNKS,)),
        ],
        compiler_params=pltpu.CompilerParams(vmem_limit_bytes=52 * 1024 * 1024),
    )(place, own, other, start, end, whole)


def places(order):
    return pl.pallas_call(
        places_kernel,
        out_shape=(jax.ShapeDtypeStruct((2, 256, 256), jnp.bfloat16),) * 2,
        in_specs=[VMEM],
        out_specs=[VMEM, VMEM],
        compiler_params=LIMIT,
    )(order)


def gram_kernel(core_ref, m_ref, mine_ref, theirs_ref):
    parts = [split(jnp.concatenate([m_ref[2 * a], m_ref[2 * a + 1]], axis=1), 2) for a in range(2)]

    def product(left, right):
        (lh, ll), (rh, rl) = left, right
        small = (short_dot(lh, rl, TN) + short_dot(ll, rh, TN)) + short_dot(ll, rl, TN)
        return short_dot(lh, rh, TN) + small

    low, high = slice(0, 128), slice(128, 256)
    blocks = []
    for part in parts:
        whole = product(part, part)
        blocks += [whole[low, low], whole[low, high], whole[high, high]]
    between = product(*parts)
    blocks += [between[low, low], between[low, high], between[high, low], between[high, high]]
    for core, halves in enumerate(((mine_ref, theirs_ref), (theirs_ref, mine_ref))):

        @pl.when(core_ref[0] == core)
        def _(halves=halves):
            for i, block in enumerate(blocks):
                halves[i // 5][i % 5] = block


def grams(core_index, blocks):
    return pl.pallas_call(
        gram_kernel,
        out_shape=(jax.ShapeDtypeStruct((5, 128, 128), jnp.float32),) * 2,
        in_specs=[SMEM, VMEM],
        out_specs=[VMEM, VMEM],
        compiler_params=LIMIT,
    )(core_index, blocks)


def exchange(parts, axes):
    return lax.all_to_all(parts, axes, 0, 0, tiled=True)


def sum_part(value, axes):
    count = lax.axis_size(axes)
    return exchange(value.reshape(count, value.shape[0] // count, 128), axes).sum(0)


def collect(value, axes):
    return exchange(jnp.broadcast_to(value[None], (lax.axis_size(axes), *value.shape)), axes)


def swap_cores(value):
    return lax.ppermute(value, "core", ((0, 1), (1, 0)))


def local(matrix, order):
    place = jnp.stack([lax.axis_index("x"), lax.axis_index("core")]).astype(jnp.int32)
    start, end = places(order)
    blocks = exchange(matrix.reshape(4, 512, 128), "x")
    matrix, blocks = lax.optimization_barrier((matrix, blocks))
    whole = lax.all_gather(matrix, "x")
    mine, theirs = grams(place[1:], blocks)
    gram = (mine + swap_cores(theirs)).reshape(640, 128)
    gram = collect(sum_part(gram, ("y", "x")), "z").sum(0)
    own = collect(gram, ("y", "x")).reshape(5, 128, 128)
    density, rms = rotate(place, own, swap_cores(own), start, end, whole)
    return density, rms.reshape(128)


def solution(mesh):
    fine = Mesh(mesh.devices.reshape(8, 8, 2, 4), ("z", "y", "core", "x"))
    rows = ("z", "y", "core")
    return jax.shard_map(
        local,
        mesh=fine,
        in_specs=(P(rows, "x"), P()),
        out_specs=(P(rows, "x"), P("x")),
        check_vma=False,
    )
```

```python
import jax
import jax.numpy as jnp
from jax import lax
from jax.experimental import pallas as pl
from jax.experimental.pallas import tpu as pltpu
from jax.sharding import Mesh, PartitionSpec as P

ROUNDS = 16
ROWS = 262144
EPS = 1e-06
HIGHEST = lax.Precision.HIGHEST
NN = (((1,), (0,)), ((), ()))
NT = (((1,), (1,)), ((), ()))
TN = (((0,), (0,)), ((), ()))
PAIRS = ((0, 0), (0, 1), (1, 1), (2, 2), (2, 3), (3, 3), (0, 2), (0, 3), (1, 2), (1, 3))
LIMIT = pltpu.CompilerParams(vmem_limit_bytes=48 * 1024 * 1024)
VMEM = pl.BlockSpec(memory_space=pltpu.VMEM)
SMEM = pl.BlockSpec(memory_space=pltpu.SMEM)
HBM = pl.BlockSpec(memory_space=pltpu.HBM)
CHUNKS = 4


def dot(a, b, dims=NN):
    return lax.dot_general(a, b, dims, precision=HIGHEST, preferred_element_type=jnp.float32)


def short_dot(a, b, dims=NN):
    return lax.dot_general(a, b, dims, preferred_element_type=jnp.float32)


def split(value, count):
    parts = []
    for _ in range(count):
        part = value.astype(jnp.bfloat16)
        value = value - part.astype(jnp.float32)
        parts.append(part)
    return parts


def pick(onehot, value, dims=NN):
    high, mid, low = (short_dot(onehot, part, dims) for part in split(value, 3))
    return high + (mid + low)


def slot_at(place, turn):
    side, inner = place // 128, place % 128
    k = 16 * (inner % 8) + inner // 8
    moved = jnp.where(side == 0, turn + k, turn + 255 - k)
    moved = jnp.where(moved >= 255, moved - 255, moved)
    return jnp.where((side == 0) & (k == 0), 255, moved)


def places_kernel(order_ref, start_ref, end_ref):
    rows = lax.broadcasted_iota(jnp.int32, (256, 256), 0)
    cols = lax.broadcasted_iota(jnp.int32, (256, 256), 1)
    first = (slot_at(rows, 0) == cols).astype(jnp.bfloat16)
    last = (slot_at(rows, ROUNDS) == cols).astype(jnp.bfloat16)
    for step in range(2):
        column_slot = (rows == order_ref[step : step + 1, :]).astype(jnp.bfloat16)
        start_ref[step] = short_dot(first, column_slot, NT).astype(jnp.bfloat16)
        end_ref[step] = short_dot(column_slot, last, NT).astype(jnp.bfloat16)


def rotation(cross, low, high):
    x = high - low
    y = cross + cross
    ax = jnp.abs(x)
    yy = y * y
    hh = x * x + yy + 1e-37
    h = hh * lax.rsqrt(hh)
    w = h + ax
    n = lax.rsqrt(w * w + yy)
    big = w * n
    small = y * n
    gap = h * small * small
    back = x < 0.0
    cs = jnp.where(back, small, big)
    sn = jnp.where(back, big, small)
    return cs, sn, jnp.minimum(low, high) - gap, jnp.maximum(low, high) + gap


def one_round(count, src, dst, dsrc, ddst, cbuf, sbuf):
    row8 = lax.broadcasted_iota(jnp.int32, (8, 128), 0)
    first, last = row8 == 0, row8 == 7

    def put(buf, lead, new):
        top, bottom = new
        for t in range(15):
            tile = top[t + 1] if t else jnp.where(first, top[0], top[1])
            buf[(*lead[0], pl.ds(8 * t, 8))] = tile
            buf[(*lead[1], pl.ds(8 * t + 8, 8))] = bottom[t]
        buf[(*lead[0], pl.ds(120, 8))] = jnp.where(last, bottom[15], pltpu.roll(top[0], 7, 0))
        buf[(*lead[1], pl.ds(0, 8))] = jnp.where(first, top[1], pltpu.roll(bottom[15], 1, 0))

    for a in range(count):
        top, bottom = [], []
        for t in range(16):
            rows = pl.ds(8 * t, 8)
            part = src[a, 0, 0, rows] * src[a, 1, 2, rows] + src[a, 0, 1, rows] * src[a, 1, 3, rows]
            cross = jnp.broadcast_to(jnp.sum(part, axis=1, keepdims=True), (8, 128))
            cs, sn, low, high = rotation(cross, dsrc[a, 0, rows], dsrc[a, 1, rows])
            cbuf[a, rows] = cs
            sbuf[a, rows] = sn
            top.append(low)
            bottom.append(high)
        put(ddst, ((a, 0), (a, 1)), (top, bottom))
    for a in range(count):
        for lane in range(4):
            top, bottom = [], []
            for t in range(16):
                rows = pl.ds(8 * t, 8)
                cs, sn = cbuf[a, rows], sbuf[a, rows]
                p, q = src[a, 0, lane, rows], src[a, 1, lane, rows]
                top.append(cs * p - sn * q)
                bottom.append(sn * p + cs * q)
            put(dst, ((a, 0, lane), (a, 1, lane)), (top, bottom))


def rotate_kernel(
    place_ref, own_ref, other_ref, start_ref, end_ref, whole_ref, out_ref, rms_ref,
    g_ref, xa, xb, da, db, cbuf, sbuf, held_rows, squares, in_sems, out_sems,
):
    rows_each = held_rows.shape[2]
    fetch = []
    for i in range(CHUNKS):
        rows = pl.ds(i * rows_each, rows_each)
        fetch.append(pltpu.make_async_copy(whole_ref.at[:, rows, :], held_rows.at[i], in_sems.at[i]))
        fetch[-1].start()
    core = place_ref[1]
    g_ref[pl.ds(5 * core, 5)] = own_ref[...]
    g_ref[pl.ds(5 * (1 - core), 5)] = other_ref[...]
    own_pair, own_side = place_ref[0] % 2, place_ref[0] // 2
    half = pl.ds(pl.multiple_of(128 * own_pair, 128), 128)

    def solve(grams, step):
        start = start_ref[step]
        start32 = start.astype(jnp.float32)
        for a, gram in enumerate(grams):
            held = pick(start, gram)
            diag = jnp.broadcast_to(jnp.sum(start32 * held, axis=1, keepdims=True), (256, 128))
            for side in range(2):
                rows = slice(128 * side, 128 * side + 128)
                da[a, side] = diag[rows]
                for lane in range(2):
                    cols = slice(128 * lane, 128 * lane + 128)
                    xa[a, side, lane] = start32[rows, cols]
                    xa[a, side, lane + 2] = held[rows, cols]

        def two_rounds(_, carry):
            one_round(len(grams), xa, xb, da, db, cbuf, sbuf)
            one_round(len(grams), xb, xa, db, da, cbuf, sbuf)
            return carry

        lax.fori_loop(0, ROUNDS // 2, two_rounds, 0)

    def placed(a, lanes):
        sides = [jnp.concatenate([xa[a, side, lane] for lane in lanes], axis=1) for side in range(2)]
        return jnp.concatenate(sides, axis=0)

    def square(a, b, d):
        return jnp.concatenate([jnp.concatenate([a, b], axis=1), jnp.concatenate([b.T, d], axis=1)], axis=0)

    solve([square(g_ref[i], g_ref[i + 1], g_ref[i + 2]) for i in (0, 3)], 0)
    end = end_ref[0, half, :]
    both = [pick(end, placed(a, range(4))) for a in range(2)]
    basis = [value[:, :256] for value in both]
    turned = [dot(value[:, :256], value[:, 256:], NT) for value in both]
    between = jnp.concatenate(
        [jnp.concatenate([g_ref[6], g_ref[7]], axis=1), jnp.concatenate([g_ref[8], g_ref[9]], axis=1)], axis=0
    )
    cross = dot(dot(basis[0], between), basis[1], NT)
    solve([square(turned[0], cross, turned[1])], 1)
    end = end_ref[1, pl.ds(pl.multiple_of(128 * own_side, 128), 128), :]
    last = pick(end, placed(0, range(2)))
    turns = jnp.concatenate([dot(last[:, :128], basis[0]), dot(last[:, 128:], basis[1])], axis=1)
    diag = jnp.concatenate([da[0, 0], da[0, 1]], axis=0)
    sums = sum(short_dot(part[:, :8], end, (((0,), (1,)), ((), ()))) for part in reversed(split(diag, 3)))
    rms_ref[...] = jnp.sqrt(jnp.maximum(sums[:1], 0.0) / ROWS + EPS)
    turn_high, turn_low = split(turns, 2)
    both = jnp.concatenate([turn_high, turn_low], axis=0)
    store = []
    for i in range(CHUNKS):
        fetch[i].wait()
        high, low = split(jnp.concatenate([held_rows[i, c] for c in range(4)], axis=1), 2)
        wide = short_dot(high, both, NT)
        value = wide[:, :128] + (wide[:, 128:] + short_dot(low, turn_high, NT))
        rows = pl.ds(i * rows_each, rows_each)
        squares[rows, :] = value * value
        store.append(pltpu.make_async_copy(squares.at[rows, :], out_ref.at[rows, :], out_sems.at[i]))
        store[-1].start()
    for copy in store:
        copy.wait()


def rotate(place, own, other, start, end, whole):
    rows = whole.shape[1]
    return pl.pallas_call(
        rotate_kernel,
        out_shape=(
            jax.ShapeDtypeStruct((rows, 128), jnp.float32),
            jax.ShapeDtypeStruct((1, 128), jnp.float32),
        ),
        in_specs=[SMEM, VMEM, VMEM, VMEM, VMEM, HBM],
        out_specs=[HBM, VMEM],
        scratch_shapes=[
            pltpu.VMEM((10, 128, 128), jnp.float32),
            pltpu.VMEM((2, 2, 4, 128, 128), jnp.float32),
            pltpu.VMEM((2, 2, 4, 128, 128), jnp.float32),
            pltpu.VMEM((2, 2, 128, 128), jnp.float32),
            pltpu.VMEM((2, 2, 128, 128), jnp.float32),
            pltpu.VMEM((2, 128, 128), jnp.float32),
            pltpu.VMEM((2, 128, 128), jnp.float32),
            pltpu.VMEM((CHUNKS, 4, rows // CHUNKS, 128), jnp.float32),
            pltpu.VMEM((rows, 128), jnp.float32),
            pltpu.SemaphoreType.DMA((CHUNKS,)),
            pltpu.SemaphoreType.DMA((CHUNKS,)),
        ],
        compiler_params=pltpu.CompilerParams(vmem_limit_bytes=52 * 1024 * 1024),
    )(place, own, other, start, end, whole)


def places(order):
    return pl.pallas_call(
        places_kernel,
        out_shape=(jax.ShapeDtypeStruct((2, 256, 256), jnp.bfloat16),) * 2,
        in_specs=[VMEM],
        out_specs=[VMEM, VMEM],
        compiler_params=LIMIT,
    )(order)


def gram_kernel(core_ref, m_ref, mine_ref, theirs_ref):
    parts = [split(jnp.concatenate([m_ref[2 * a], m_ref[2 * a + 1]], axis=1), 2) for a in range(2)]

    def product(left, right):
        (lh, ll), (rh, rl) = left, right
        small = (short_dot(lh, rl, TN) + short_dot(ll, rh, TN)) + short_dot(ll, rl, TN)
        return short_dot(lh, rh, TN) + small

    low, high = slice(0, 128), slice(128, 256)
    blocks = []
    for part in parts:
        whole = product(part, part)
        blocks += [whole[low, low], whole[low, high], whole[high, high]]
    between = product(*parts)
    blocks += [between[low, low], between[low, high], between[high, low], between[high, high]]
    for core, halves in enumerate(((mine_ref, theirs_ref), (theirs_ref, mine_ref))):

        @pl.when(core_ref[0] == core)
        def _(halves=halves):
            for i, block in enumerate(blocks):
                halves[i // 5][i % 5] = block


def grams(core_index, blocks):
    return pl.pallas_call(
        gram_kernel,
        out_shape=(jax.ShapeDtypeStruct((5, 128, 128), jnp.float32),) * 2,
        in_specs=[SMEM, VMEM],
        out_specs=[VMEM, VMEM],
        compiler_params=LIMIT,
    )(core_index, blocks)


def exchange(parts, axes):
    return lax.all_to_all(parts, axes, 0, 0, tiled=True)


def sum_part(value, axes):
    count = lax.axis_size(axes)
    return exchange(value.reshape(count, 1, value.size // count), axes).sum(0)


def collect(value, axes):
    return exchange(jnp.broadcast_to(value[None], (lax.axis_size(axes), *value.shape)), axes)


def swap_cores(value):
    return lax.ppermute(value, "core", ((0, 1), (1, 0)))


def local(matrix, order):
    place = jnp.stack([lax.axis_index("x"), lax.axis_index("core")]).astype(jnp.int32)
    start, end = places(order)
    blocks = exchange(matrix.reshape(4, 512, 128), "x")
    matrix, blocks = lax.optimization_barrier((matrix, blocks))
    whole = lax.all_gather(matrix, "x")
    mine, theirs = grams(place[1:], blocks)
    gram = (mine + swap_cores(theirs)).reshape(640, 128)
    gram = collect(sum_part(gram, ("y", "x")), "z").sum(0)
    own = collect(gram, ("y", "x")).reshape(5, 128, 128)
    density, rms = rotate(place, own, swap_cores(own), start, end, whole)
    return density, rms.reshape(128)


def solution(mesh):
    fine = Mesh(mesh.devices.reshape(8, 8, 2, 4), ("z", "y", "core", "x"))
    rows = ("z", "y", "core")
    return jax.shard_map(
        local,
        mesh=fine,
        in_specs=(P(rows, "x"), P()),
        out_specs=(P(rows, "x"), P("x")),
        check_vma=False,
    )
```

```python
import jax
import jax.numpy as jnp
from jax import lax
from jax.experimental import pallas as pl
from jax.experimental.pallas import tpu as pltpu
from jax.sharding import Mesh, PartitionSpec as P

ROUNDS = 16
ROWS = 262144
EPS = 1e-06
HIGHEST = lax.Precision.HIGHEST
NN = (((1,), (0,)), ((), ()))
NT = (((1,), (1,)), ((), ()))
TN = (((0,), (0,)), ((), ()))
HALF_ROWS = 544
LIMIT = pltpu.CompilerParams(vmem_limit_bytes=48 * 1024 * 1024)
VMEM = pl.BlockSpec(memory_space=pltpu.VMEM)
SMEM = pl.BlockSpec(memory_space=pltpu.SMEM)
HBM = pl.BlockSpec(memory_space=pltpu.HBM)
CHUNKS = 4


def dot(a, b, dims=NN):
    return lax.dot_general(a, b, dims, precision=HIGHEST, preferred_element_type=jnp.float32)


def short_dot(a, b, dims=NN):
    return lax.dot_general(a, b, dims, preferred_element_type=jnp.float32)


def split(value, count):
    parts = []
    for _ in range(count):
        part = value.astype(jnp.bfloat16)
        value = value - part.astype(jnp.float32)
        parts.append(part)
    return parts


def pick(onehot, value, dims=NN):
    high, mid, low = (short_dot(onehot, part, dims) for part in split(value, 3))
    return high + (mid + low)


def slot_at(place, turn):
    side, inner = place // 128, place % 128
    k = 16 * (inner % 8) + inner // 8
    moved = jnp.where(side == 0, turn + k, turn + 255 - k)
    moved = jnp.where(moved >= 255, moved - 255, moved)
    return jnp.where((side == 0) & (k == 0), 255, moved)


def places_kernel(order_ref, start_ref, end_ref):
    rows = lax.broadcasted_iota(jnp.int32, (256, 256), 0)
    cols = lax.broadcasted_iota(jnp.int32, (256, 256), 1)
    first = (slot_at(rows, 0) == cols).astype(jnp.bfloat16)
    last = (slot_at(rows, ROUNDS) == cols).astype(jnp.bfloat16)
    for step in range(2):
        column_slot = (rows == order_ref[step : step + 1, :]).astype(jnp.bfloat16)
        start_ref[step] = short_dot(first, column_slot, NT).astype(jnp.bfloat16)
        end_ref[step] = short_dot(column_slot, last, NT).astype(jnp.bfloat16)


def rotation(cross, low, high):
    x = high - low
    y = cross + cross
    ax = jnp.abs(x)
    yy = y * y
    hh = x * x + yy + 1e-37
    h = hh * lax.rsqrt(hh)
    w = h + ax
    n = lax.rsqrt(w * w + yy)
    big = w * n
    small = y * n
    gap = h * small * small
    back = x < 0.0
    cs = jnp.where(back, small, big)
    sn = jnp.where(back, big, small)
    return cs, sn, jnp.minimum(low, high) - gap, jnp.maximum(low, high) + gap


def one_round(count, src, dst, dsrc, ddst, cbuf, sbuf):
    row8 = lax.broadcasted_iota(jnp.int32, (8, 128), 0)
    first, last = row8 == 0, row8 == 7

    def put(buf, lead, new):
        top, bottom = new
        for t in range(15):
            tile = top[t + 1] if t else jnp.where(first, top[0], top[1])
            buf[(*lead[0], pl.ds(8 * t, 8))] = tile
            buf[(*lead[1], pl.ds(8 * t + 8, 8))] = bottom[t]
        buf[(*lead[0], pl.ds(120, 8))] = jnp.where(last, bottom[15], pltpu.roll(top[0], 7, 0))
        buf[(*lead[1], pl.ds(0, 8))] = jnp.where(first, top[1], pltpu.roll(bottom[15], 1, 0))

    for a in range(count):
        top, bottom = [], []
        for t in range(16):
            rows = pl.ds(8 * t, 8)
            part = src[a, 0, 0, rows] * src[a, 1, 2, rows] + src[a, 0, 1, rows] * src[a, 1, 3, rows]
            cross = jnp.broadcast_to(jnp.sum(part, axis=1, keepdims=True), (8, 128))
            cs, sn, low, high = rotation(cross, dsrc[a, 0, rows], dsrc[a, 1, rows])
            cbuf[a, rows] = cs
            sbuf[a, rows] = sn
            top.append(low)
            bottom.append(high)
        put(ddst, ((a, 0), (a, 1)), (top, bottom))
    for a in range(count):
        for lane in range(4):
            top, bottom = [], []
            for t in range(16):
                rows = pl.ds(8 * t, 8)
                cs, sn = cbuf[a, rows], sbuf[a, rows]
                p, q = src[a, 0, lane, rows], src[a, 1, lane, rows]
                top.append(cs * p - sn * q)
                bottom.append(sn * p + cs * q)
            put(dst, ((a, 0, lane), (a, 1, lane)), (top, bottom))


def rotate_kernel(
    place_ref, own_ref, other_ref, start_ref, end_ref, whole_ref, out_ref, rms_ref,
    g_ref, xa, xb, da, db, cbuf, sbuf, held_rows, squares, in_sems, out_sems,
):
    rows_each = held_rows.shape[2]
    fetch = []
    for i in range(CHUNKS):
        rows = pl.ds(i * rows_each, rows_each)
        fetch.append(pltpu.make_async_copy(whole_ref.at[:, rows, :], held_rows.at[i], in_sems.at[i]))
        fetch[-1].start()
    core = place_ref[1]
    g_ref[core] = own_ref[:520, :]
    g_ref[1 - core] = other_ref[:520, :]
    own_pair, own_side = place_ref[0] % 2, place_ref[0] // 2
    half = pl.ds(pl.multiple_of(128 * own_pair, 128), 128)

    def solve(grams, step):
        start = start_ref[step]
        start32 = start.astype(jnp.float32)
        for a, gram in enumerate(grams):
            held = pick(start, gram)
            diag = jnp.broadcast_to(jnp.sum(start32 * held, axis=1, keepdims=True), (256, 128))
            for side in range(2):
                rows = slice(128 * side, 128 * side + 128)
                da[a, side] = diag[rows]
                for lane in range(2):
                    cols = slice(128 * lane, 128 * lane + 128)
                    xa[a, side, lane] = start32[rows, cols]
                    xa[a, side, lane + 2] = held[rows, cols]

        def two_rounds(_, carry):
            one_round(len(grams), xa, xb, da, db, cbuf, sbuf)
            one_round(len(grams), xb, xa, db, da, cbuf, sbuf)
            return carry

        lax.fori_loop(0, ROUNDS // 2, two_rounds, 0)

    def placed(a, lanes):
        sides = [jnp.concatenate([xa[a, side, lane] for lane in lanes], axis=1) for side in range(2)]
        return jnp.concatenate(sides, axis=0)

    def unpack(i):
        row = lax.broadcasted_iota(jnp.int32, (128, 128), 0)
        col = lax.broadcasted_iota(jnp.int32, (128, 128), 1)
        packed = g_ref[i, :128, :]
        turned = packed.T
        one = jnp.where(row <= col, packed, turned)
        other = jnp.where(row > col, packed, jnp.where(row == col, g_ref[i, 512:513, :], turned))
        return square(one, g_ref[i, 128:256, :], other)

    def square(a, b, d):
        return jnp.concatenate([jnp.concatenate([a, b], axis=1), jnp.concatenate([b.T, d], axis=1)], axis=0)

    solve([unpack(i) for i in range(2)], 0)
    end = end_ref[0, half, :]
    both = [pick(end, placed(a, range(4))) for a in range(2)]
    basis = [value[:, :256] for value in both]
    turned = [dot(value[:, :256], value[:, 256:], NT) for value in both]
    between = jnp.concatenate(
        [jnp.concatenate([g_ref[i, 256:384, :], g_ref[i, 384:512, :]], axis=1) for i in range(2)], axis=0
    )
    cross = dot(dot(basis[0], between), basis[1], NT)
    solve([square(turned[0], cross, turned[1])], 1)
    end = end_ref[1, pl.ds(pl.multiple_of(128 * own_side, 128), 128), :]
    last = pick(end, placed(0, range(2)))
    turns = jnp.concatenate([dot(last[:, :128], basis[0]), dot(last[:, 128:], basis[1])], axis=1)
    diag = jnp.concatenate([da[0, 0], da[0, 1]], axis=0)
    sums = sum(short_dot(part[:, :8], end, (((0,), (1,)), ((), ()))) for part in reversed(split(diag, 3)))
    rms_ref[...] = jnp.sqrt(jnp.maximum(sums[:1], 0.0) / ROWS + EPS)
    turn_high, turn_low = split(turns, 2)
    both = jnp.concatenate([turn_high, turn_low], axis=0)
    store = []
    for i in range(CHUNKS):
        fetch[i].wait()
        high, low = split(jnp.concatenate([held_rows[i, c] for c in range(4)], axis=1), 2)
        wide = short_dot(high, both, NT)
        value = wide[:, :128] + (wide[:, 128:] + short_dot(low, turn_high, NT))
        rows = pl.ds(i * rows_each, rows_each)
        squares[rows, :] = value * value
        store.append(pltpu.make_async_copy(squares.at[rows, :], out_ref.at[rows, :], out_sems.at[i]))
        store[-1].start()
    for copy in store:
        copy.wait()


def rotate(place, own, other, start, end, whole):
    rows = whole.shape[1]
    return pl.pallas_call(
        rotate_kernel,
        out_shape=(
            jax.ShapeDtypeStruct((rows, 128), jnp.float32),
            jax.ShapeDtypeStruct((1, 128), jnp.float32),
        ),
        in_specs=[SMEM, VMEM, VMEM, VMEM, VMEM, HBM],
        out_specs=[HBM, VMEM],
        scratch_shapes=[
            pltpu.VMEM((2, 520, 128), jnp.float32),
            pltpu.VMEM((2, 2, 4, 128, 128), jnp.float32),
            pltpu.VMEM((2, 2, 4, 128, 128), jnp.float32),
            pltpu.VMEM((2, 2, 128, 128), jnp.float32),
            pltpu.VMEM((2, 2, 128, 128), jnp.float32),
            pltpu.VMEM((2, 128, 128), jnp.float32),
            pltpu.VMEM((2, 128, 128), jnp.float32),
            pltpu.VMEM((CHUNKS, 4, rows // CHUNKS, 128), jnp.float32),
            pltpu.VMEM((rows, 128), jnp.float32),
            pltpu.SemaphoreType.DMA((CHUNKS,)),
            pltpu.SemaphoreType.DMA((CHUNKS,)),
        ],
        compiler_params=pltpu.CompilerParams(vmem_limit_bytes=52 * 1024 * 1024),
    )(place, own, other, start, end, whole)


def places(order):
    return pl.pallas_call(
        places_kernel,
        out_shape=(jax.ShapeDtypeStruct((2, 256, 256), jnp.bfloat16),) * 2,
        in_specs=[VMEM],
        out_specs=[VMEM, VMEM],
        compiler_params=LIMIT,
    )(order)


def gram_kernel(core_ref, m_ref, mine_ref, theirs_ref):
    parts = [split(jnp.concatenate([m_ref[2 * a], m_ref[2 * a + 1]], axis=1), 2) for a in range(2)]

    def product(left, right):
        (lh, ll), (rh, rl) = left, right
        small = (short_dot(lh, rl, TN) + short_dot(ll, rh, TN)) + short_dot(ll, rl, TN)
        return short_dot(lh, rh, TN) + small

    low, high = slice(0, 128), slice(128, 256)
    between = product(*parts)
    row = lax.broadcasted_iota(jnp.int32, (128, 128), 0)
    col = lax.broadcasted_iota(jnp.int32, (128, 128), 1)
    halves = []
    for i, part in enumerate(parts):
        whole = product(part, part)
        own = (low, high)[i]
        diag = jnp.sum(jnp.where(row == col, whole[high, high], 0.0), axis=0, keepdims=True)
        packed = jnp.where(row <= col, whole[low, low], whole[high, high])
        blocks = [packed, whole[low, high], between[own, low], between[own, high]]
        rest = jnp.zeros((HALF_ROWS - 520, 128), jnp.float32)
        halves.append([*blocks, jnp.broadcast_to(diag, (8, 128)), rest])
    for core in range(2):

        @pl.when(core_ref[0] == core)
        def _(core=core):
            for ref, half in ((mine_ref, halves[core]), (theirs_ref, halves[1 - core])):
                at = 0
                for block in half:
                    ref[at : at + block.shape[0], :] = block
                    at += block.shape[0]


def grams(core_index, blocks):
    return pl.pallas_call(
        gram_kernel,
        out_shape=(jax.ShapeDtypeStruct((HALF_ROWS, 128), jnp.float32),) * 2,
        in_specs=[SMEM, VMEM],
        out_specs=[VMEM, VMEM],
        compiler_params=LIMIT,
    )(core_index, blocks)


def exchange(parts, axes):
    return lax.all_to_all(parts, axes, 0, 0, tiled=True)


def sum_part(value, axes):
    count = lax.axis_size(axes)
    return exchange(value.reshape(count, 1, value.size // count), axes).sum(0)


def collect(value, axes):
    return exchange(jnp.broadcast_to(value[None], (lax.axis_size(axes), *value.shape)), axes)


def swap_cores(value):
    return lax.ppermute(value, "core", ((0, 1), (1, 0)))


def local(matrix, order):
    place = jnp.stack([lax.axis_index("x"), lax.axis_index("core")]).astype(jnp.int32)
    start, end = places(order)
    blocks = exchange(matrix.reshape(4, 512, 128), "x")
    matrix, blocks = lax.optimization_barrier((matrix, blocks))
    whole = lax.all_gather(matrix, "x")
    mine, theirs = grams(place[1:], blocks)
    gram = mine + swap_cores(theirs)
    gram = collect(sum_part(gram, ("y", "x")), "z").sum(0)
    own = collect(gram, ("y", "x")).reshape(HALF_ROWS, 128)
    density, rms = rotate(place, own, swap_cores(own), start, end, whole)
    return density, rms.reshape(128)


def solution(mesh):
    fine = Mesh(mesh.devices.reshape(8, 8, 2, 4), ("z", "y", "core", "x"))
    rows = ("z", "y", "core")
    return jax.shard_map(
        local,
        mesh=fine,
        in_specs=(P(rows, "x"), P()),
        out_specs=(P(rows, "x"), P("x")),
        check_vma=False,
    )
```

```python
import jax
import jax.numpy as jnp
from jax import lax
from jax.experimental import pallas as pl
from jax.experimental.pallas import tpu as pltpu
from jax.sharding import Mesh, PartitionSpec as P

ROUNDS = 16
ROWS = 262144
EPS = 1e-06
HIGHEST = lax.Precision.HIGHEST
NN = (((1,), (0,)), ((), ()))
NT = (((1,), (1,)), ((), ()))
TN = (((0,), (0,)), ((), ()))
HALF_ROWS = 544
LIMIT = pltpu.CompilerParams(vmem_limit_bytes=48 * 1024 * 1024)
VMEM = pl.BlockSpec(memory_space=pltpu.VMEM)
SMEM = pl.BlockSpec(memory_space=pltpu.SMEM)
HBM = pl.BlockSpec(memory_space=pltpu.HBM)
CHUNKS = 4


def dot(a, b, dims=NN):
    return lax.dot_general(a, b, dims, precision=HIGHEST, preferred_element_type=jnp.float32)


def short_dot(a, b, dims=NN):
    return lax.dot_general(a, b, dims, preferred_element_type=jnp.float32)


def split(value, count):
    parts = []
    for _ in range(count):
        part = value.astype(jnp.bfloat16)
        value = value - part.astype(jnp.float32)
        parts.append(part)
    return parts


def pick(onehot, value, dims=NN):
    high, mid, low = (short_dot(onehot, part, dims) for part in split(value, 3))
    return high + (mid + low)


def slot_at(place, turn):
    side, inner = place // 128, place % 128
    k = 16 * (inner % 8) + inner // 8
    moved = jnp.where(side == 0, turn + k, turn + 255 - k)
    moved = jnp.where(moved >= 255, moved - 255, moved)
    return jnp.where((side == 0) & (k == 0), 255, moved)


def places_kernel(order_ref, start_ref, end_ref):
    rows = lax.broadcasted_iota(jnp.int32, (256, 256), 0)
    cols = lax.broadcasted_iota(jnp.int32, (256, 256), 1)
    first = (slot_at(rows, 0) == cols).astype(jnp.bfloat16)
    last = (slot_at(rows, ROUNDS) == cols).astype(jnp.bfloat16)
    for step in range(2):
        column_slot = (rows == order_ref[step : step + 1, :]).astype(jnp.bfloat16)
        start_ref[step] = short_dot(first, column_slot, NT).astype(jnp.bfloat16)
        end_ref[step] = short_dot(column_slot, last, NT).astype(jnp.bfloat16)


def rotation(cross, low, high):
    x = high - low
    y = cross + cross
    ax = jnp.abs(x)
    yy = y * y
    hh = x * x + yy + 1e-37
    h = hh * lax.rsqrt(hh)
    w = h + ax
    n = lax.rsqrt(w * w + yy)
    big = w * n
    small = y * n
    gap = h * small * small
    back = x < 0.0
    cs = jnp.where(back, small, big)
    sn = jnp.where(back, big, small)
    return cs, sn, jnp.minimum(low, high) - gap, jnp.maximum(low, high) + gap


def one_round(src, dst, dsrc, ddst, cbuf, sbuf):
    row8 = lax.broadcasted_iota(jnp.int32, (8, 128), 0)
    first, last = row8 == 0, row8 == 7

    def put(tops, bottoms, top, bottom):
        for t in range(15):
            tops[pl.ds(8 * t, 8)] = top[t + 1] if t else jnp.where(first, top[0], top[1])
            bottoms[pl.ds(8 * t + 8, 8)] = bottom[t]
        tops[pl.ds(120, 8)] = jnp.where(last, bottom[15], pltpu.roll(top[0], 7, 0))
        bottoms[pl.ds(0, 8)] = jnp.where(first, top[1], pltpu.roll(bottom[15], 1, 0))

    top, bottom = [], []
    for t in range(16):
        rows = pl.ds(8 * t, 8)
        part = src[0, 0, rows] * src[1, 2, rows] + src[0, 1, rows] * src[1, 3, rows]
        cross = jnp.broadcast_to(jnp.sum(part, axis=1, keepdims=True), (8, 128))
        cs, sn, low, high = rotation(cross, dsrc[0, rows], dsrc[1, rows])
        cbuf[rows] = cs
        sbuf[rows] = sn
        top.append(low)
        bottom.append(high)
    put(ddst.at[0], ddst.at[1], top, bottom)
    for lane in range(4):
        top, bottom = [], []
        for t in range(16):
            rows = pl.ds(8 * t, 8)
            cs, sn = cbuf[rows], sbuf[rows]
            p, q = src[0, lane, rows], src[1, lane, rows]
            top.append(cs * p - sn * q)
            bottom.append(sn * p + cs * q)
        put(dst.at[0, lane], dst.at[1, lane], top, bottom)


TURNING = [
    pltpu.VMEM((2, 4, 128, 128), jnp.float32),
    pltpu.VMEM((2, 4, 128, 128), jnp.float32),
    pltpu.VMEM((2, 128, 128), jnp.float32),
    pltpu.VMEM((2, 128, 128), jnp.float32),
    pltpu.VMEM((128, 128), jnp.float32),
    pltpu.VMEM((128, 128), jnp.float32),
]


def turn(gram, start, xa, xb, da, db, cbuf, sbuf):
    start32 = start.astype(jnp.float32)
    held = pick(start, gram)
    diag = jnp.broadcast_to(jnp.sum(start32 * held, axis=1, keepdims=True), (256, 128))
    for side in range(2):
        rows = slice(128 * side, 128 * side + 128)
        da[side] = diag[rows]
        for lane in range(2):
            cols = slice(128 * lane, 128 * lane + 128)
            xa[side, lane] = start32[rows, cols]
            xa[side, lane + 2] = held[rows, cols]

    def two_rounds(_, carry):
        one_round(xa, xb, da, db, cbuf, sbuf)
        one_round(xb, xa, db, da, cbuf, sbuf)
        return carry

    lax.fori_loop(0, ROUNDS // 2, two_rounds, 0, unroll=True)


def placed(xa, lanes):
    sides = [jnp.concatenate([xa[side, lane] for lane in lanes], axis=1) for side in range(2)]
    return jnp.concatenate(sides, axis=0)


def square(a, b, d):
    return jnp.concatenate([jnp.concatenate([a, b], axis=1), jnp.concatenate([b.T, d], axis=1)], axis=0)


def first_kernel(place_ref, half_ref, start_ref, end_ref, out_ref, *turning):
    row = lax.broadcasted_iota(jnp.int32, (128, 128), 0)
    col = lax.broadcasted_iota(jnp.int32, (128, 128), 1)
    packed = half_ref[:128, :]
    mirrored = packed.T
    one = jnp.where(row <= col, packed, mirrored)
    other = jnp.where(row > col, packed, jnp.where(row == col, half_ref[512:513, :], mirrored))
    turn(square(one, half_ref[128:256, :], other), start_ref[0], *turning)
    own_pair = place_ref[0] % 2
    end = end_ref[0, pl.ds(pl.multiple_of(128 * own_pair, 128), 128), :]
    both = pick(end, placed(turning[0], range(4)))
    out_ref[:128, :] = both[:, :128]
    out_ref[128:256, :] = both[:, 128:256]
    out_ref[256:384, :] = dot(both[:, :256], both[:, 256:], NT)
    out_ref[384:, :] = half_ref[256:512, :]


def first_turns(place, half, start, end):
    return pl.pallas_call(
        first_kernel,
        out_shape=jax.ShapeDtypeStruct((640, 128), jnp.float32),
        in_specs=[SMEM, VMEM, VMEM, VMEM],
        out_specs=VMEM,
        scratch_shapes=TURNING,
        compiler_params=LIMIT,
    )(place, half, start, end)


def second_kernel(
    place_ref, own_ref, other_ref, start_ref, end_ref, whole_ref, out_ref, rms_ref,
    g_ref, held_rows, squares, in_sem, out_sems, *turning,
):
    fetch = pltpu.make_async_copy(whole_ref, held_rows, in_sem)
    fetch.start()
    core = place_ref[1]
    g_ref[core] = own_ref[...]
    g_ref[1 - core] = other_ref[...]
    basis = [jnp.concatenate([g_ref[i, :128, :], g_ref[i, 128:256, :]], axis=1) for i in range(2)]
    between = jnp.concatenate(
        [jnp.concatenate([g_ref[i, 384:512, :], g_ref[i, 512:640, :]], axis=1) for i in range(2)], axis=0
    )
    cross = dot(dot(basis[0], between), basis[1], NT)
    turn(square(g_ref[0, 256:384, :], cross, g_ref[1, 256:384, :]), start_ref[1], *turning)
    own_side = place_ref[0] // 2
    end = end_ref[1, pl.ds(pl.multiple_of(128 * own_side, 128), 128), :]
    last = pick(end, placed(turning[0], range(2)))
    turns = jnp.concatenate([dot(last[:, :128], basis[0]), dot(last[:, 128:], basis[1])], axis=1)
    diag = jnp.concatenate([turning[2][0], turning[2][1]], axis=0)
    sums = sum(short_dot(part[:, :8], end, (((0,), (1,)), ((), ()))) for part in reversed(split(diag, 3)))
    rms_ref[...] = jnp.sqrt(jnp.maximum(sums[:1], 0.0) / ROWS + EPS)
    turn_high, turn_low = split(turns, 2)
    both = jnp.concatenate([turn_high, turn_low], axis=0)
    fetch.wait()
    rows_each = held_rows.shape[1] // CHUNKS
    store = []
    for i in range(CHUNKS):
        rows = pl.ds(i * rows_each, rows_each)
        high, low = split(jnp.concatenate([held_rows[c, rows] for c in range(4)], axis=1), 2)
        wide = short_dot(high, both, NT)
        value = wide[:, :128] + (wide[:, 128:] + short_dot(low, turn_high, NT))
        squares[rows, :] = value * value
        store.append(pltpu.make_async_copy(squares.at[rows, :], out_ref.at[rows, :], out_sems.at[i]))
        store[-1].start()
    for copy in store:
        copy.wait()


def second_turns(place, own, other, start, end, whole):
    rows = whole.shape[1]
    return pl.pallas_call(
        second_kernel,
        out_shape=(
            jax.ShapeDtypeStruct((rows, 128), jnp.float32),
            jax.ShapeDtypeStruct((1, 128), jnp.float32),
        ),
        in_specs=[SMEM, VMEM, VMEM, VMEM, VMEM, HBM],
        out_specs=[HBM, VMEM],
        scratch_shapes=[
            pltpu.VMEM((2, 640, 128), jnp.float32),
            pltpu.VMEM((4, rows, 128), jnp.float32),
            pltpu.VMEM((rows, 128), jnp.float32),
            pltpu.SemaphoreType.DMA,
            pltpu.SemaphoreType.DMA((CHUNKS,)),
            *TURNING,
        ],
        compiler_params=pltpu.CompilerParams(vmem_limit_bytes=52 * 1024 * 1024),
    )(place, own, other, start, end, whole)


def places(order):
    return pl.pallas_call(
        places_kernel,
        out_shape=(jax.ShapeDtypeStruct((2, 256, 256), jnp.bfloat16),) * 2,
        in_specs=[VMEM],
        out_specs=[VMEM, VMEM],
        compiler_params=LIMIT,
    )(order)


def gram_kernel(core_ref, m_ref, mine_ref, theirs_ref):
    parts = [split(jnp.concatenate([m_ref[2 * a], m_ref[2 * a + 1]], axis=1), 2) for a in range(2)]

    def product(left, right):
        (lh, ll), (rh, rl) = left, right
        small = (short_dot(lh, rl, TN) + short_dot(ll, rh, TN)) + short_dot(ll, rl, TN)
        return short_dot(lh, rh, TN) + small

    low, high = slice(0, 128), slice(128, 256)
    between = product(*parts)
    row = lax.broadcasted_iota(jnp.int32, (128, 128), 0)
    col = lax.broadcasted_iota(jnp.int32, (128, 128), 1)
    halves = []
    for i, part in enumerate(parts):
        whole = product(part, part)
        own = (low, high)[i]
        diag = jnp.sum(jnp.where(row == col, whole[high, high], 0.0), axis=0, keepdims=True)
        packed = jnp.where(row <= col, whole[low, low], whole[high, high])
        blocks = [packed, whole[low, high], between[own, low], between[own, high]]
        rest = jnp.zeros((HALF_ROWS - 520, 128), jnp.float32)
        halves.append([*blocks, jnp.broadcast_to(diag, (8, 128)), rest])
    for core in range(2):

        @pl.when(core_ref[0] == core)
        def _(core=core):
            for ref, half in ((mine_ref, halves[core]), (theirs_ref, halves[1 - core])):
                at = 0
                for block in half:
                    ref[at : at + block.shape[0], :] = block
                    at += block.shape[0]


def grams(core_index, blocks):
    return pl.pallas_call(
        gram_kernel,
        out_shape=(jax.ShapeDtypeStruct((HALF_ROWS, 128), jnp.float32),) * 2,
        in_specs=[SMEM, VMEM],
        out_specs=[VMEM, VMEM],
        compiler_params=LIMIT,
    )(core_index, blocks)


def exchange(parts, axes):
    return lax.all_to_all(parts, axes, 0, 0, tiled=True)


def sum_part(value, axes):
    count = lax.axis_size(axes)
    return exchange(value.reshape(count, 1, value.size // count), axes).sum(0)


def collect(value, axes):
    return exchange(jnp.broadcast_to(value[None], (lax.axis_size(axes), *value.shape)), axes)


def swap_cores(value):
    return lax.ppermute(value, "core", ((0, 1), (1, 0)))


def local(matrix, order):
    place = jnp.stack([lax.axis_index("x"), lax.axis_index("core")]).astype(jnp.int32)
    blocks = exchange(matrix.reshape(4, 512, 128), "x")
    matrix, blocks = lax.optimization_barrier((matrix, blocks))
    whole = lax.all_gather(matrix, "x")
    mine, theirs = grams(place[1:], blocks)
    theirs, place, start, end = lax.optimization_barrier((swap_cores(theirs), place, *places(order)))
    gram = mine + theirs
    gram = collect(sum_part(gram, ("y", "x")), "z").sum(0)
    half = collect(gram, ("y", "x")).reshape(HALF_ROWS, 128)
    own = first_turns(place, half, start, end)
    density, rms = second_turns(place, own, swap_cores(own), start, end, whole)
    return density, rms.reshape(128)


def solution(mesh):
    fine = Mesh(mesh.devices.reshape(8, 8, 2, 4), ("z", "y", "core", "x"))
    rows = ("z", "y", "core")
    return jax.shard_map(
        local,
        mesh=fine,
        in_specs=(P(rows, "x"), P()),
        out_specs=(P(rows, "x"), P("x")),
        check_vma=False,
    )
```

```python
import jax
import jax.numpy as jnp
from jax import lax
from jax.experimental import pallas as pl
from jax.experimental.pallas import tpu as pltpu
from jax.sharding import Mesh, PartitionSpec as P

ROUNDS = 16
ROWS = 262144
EPS = 1e-06
HIGHEST = lax.Precision.HIGHEST
NN = (((1,), (0,)), ((), ()))
NT = (((1,), (1,)), ((), ()))
TN = (((0,), (0,)), ((), ()))
HALF_ROWS = 544
LIMIT = pltpu.CompilerParams(vmem_limit_bytes=48 * 1024 * 1024)
VMEM = pl.BlockSpec(memory_space=pltpu.VMEM)
SMEM = pl.BlockSpec(memory_space=pltpu.SMEM)
HBM = pl.BlockSpec(memory_space=pltpu.HBM)
QUARTER = 512


def dot(a, b, dims=NN):
    return lax.dot_general(a, b, dims, precision=HIGHEST, preferred_element_type=jnp.float32)


def short_dot(a, b, dims=NN):
    return lax.dot_general(a, b, dims, preferred_element_type=jnp.float32)


def split(value, count):
    parts = []
    for _ in range(count):
        part = value.astype(jnp.bfloat16)
        value = value - part.astype(jnp.float32)
        parts.append(part)
    return parts


def pick(onehot, value, dims=NN):
    high, mid, low = (short_dot(onehot, part, dims) for part in split(value, 3))
    return high + (mid + low)


def slot_at(place, turn):
    side, inner = place // 128, place % 128
    k = 16 * (inner % 8) + inner // 8
    moved = jnp.where(side == 0, turn + k, turn + 255 - k)
    moved = jnp.where(moved >= 255, moved - 255, moved)
    return jnp.where((side == 0) & (k == 0), 255, moved)


def places_kernel(order_ref, start_ref, end_ref):
    rows = lax.broadcasted_iota(jnp.int32, (256, 256), 0)
    cols = lax.broadcasted_iota(jnp.int32, (256, 256), 1)
    first = (slot_at(rows, 0) == cols).astype(jnp.bfloat16)
    last = (slot_at(rows, ROUNDS) == cols).astype(jnp.bfloat16)
    for step in range(2):
        column_slot = (rows == order_ref[step : step + 1, :]).astype(jnp.bfloat16)
        start_ref[step] = short_dot(first, column_slot, NT).astype(jnp.bfloat16)
        end_ref[step] = short_dot(column_slot, last, NT).astype(jnp.bfloat16)


def rotation(cross, low, high):
    x = high - low
    y = cross + cross
    ax = jnp.abs(x)
    yy = y * y
    hh = x * x + yy + 1e-37
    h = hh * lax.rsqrt(hh)
    w = h + ax
    n = lax.rsqrt(w * w + yy)
    big = w * n
    small = y * n
    gap = h * small * small
    back = x < 0.0
    cs = jnp.where(back, small, big)
    sn = jnp.where(back, big, small)
    return cs, sn, jnp.minimum(low, high) - gap, jnp.maximum(low, high) + gap


def one_round(src, dst, dsrc, ddst, cbuf, sbuf):
    row8 = lax.broadcasted_iota(jnp.int32, (8, 128), 0)
    first, last = row8 == 0, row8 == 7

    def put(tops, bottoms, top, bottom):
        for t in range(15):
            tops[pl.ds(8 * t, 8)] = top[t + 1] if t else jnp.where(first, top[0], top[1])
            bottoms[pl.ds(8 * t + 8, 8)] = bottom[t]
        tops[pl.ds(120, 8)] = jnp.where(last, bottom[15], pltpu.roll(top[0], 7, 0))
        bottoms[pl.ds(0, 8)] = jnp.where(first, top[1], pltpu.roll(bottom[15], 1, 0))

    top, bottom = [], []
    for t in range(16):
        rows = pl.ds(8 * t, 8)
        part = src[0, 0, rows] * src[1, 2, rows] + src[0, 1, rows] * src[1, 3, rows]
        cross = jnp.broadcast_to(jnp.sum(part, axis=1, keepdims=True), (8, 128))
        cs, sn, low, high = rotation(cross, dsrc[0, rows], dsrc[1, rows])
        cbuf[rows] = cs
        sbuf[rows] = sn
        top.append(low)
        bottom.append(high)
    put(ddst.at[0], ddst.at[1], top, bottom)
    for lane in range(4):
        top, bottom = [], []
        for t in range(16):
            rows = pl.ds(8 * t, 8)
            cs, sn = cbuf[rows], sbuf[rows]
            p, q = src[0, lane, rows], src[1, lane, rows]
            top.append(cs * p - sn * q)
            bottom.append(sn * p + cs * q)
        put(dst.at[0, lane], dst.at[1, lane], top, bottom)


TURNING = [
    pltpu.VMEM((2, 4, 128, 128), jnp.float32),
    pltpu.VMEM((2, 4, 128, 128), jnp.float32),
    pltpu.VMEM((2, 128, 128), jnp.float32),
    pltpu.VMEM((2, 128, 128), jnp.float32),
    pltpu.VMEM((128, 128), jnp.float32),
    pltpu.VMEM((128, 128), jnp.float32),
]


def turn(gram, start, xa, xb, da, db, cbuf, sbuf):
    start32 = start.astype(jnp.float32)
    held = pick(start, gram)
    diag = jnp.broadcast_to(jnp.sum(start32 * held, axis=1, keepdims=True), (256, 128))
    for side in range(2):
        rows = slice(128 * side, 128 * side + 128)
        da[side] = diag[rows]
        for lane in range(2):
            cols = slice(128 * lane, 128 * lane + 128)
            xa[side, lane] = start32[rows, cols]
            xa[side, lane + 2] = held[rows, cols]

    def two_rounds(_, carry):
        one_round(xa, xb, da, db, cbuf, sbuf)
        one_round(xb, xa, db, da, cbuf, sbuf)
        return carry

    lax.fori_loop(0, ROUNDS // 2, two_rounds, 0, unroll=True)


def placed(xa, lanes):
    sides = [jnp.concatenate([xa[side, lane] for lane in lanes], axis=1) for side in range(2)]
    return jnp.concatenate(sides, axis=0)


def square(a, b, d):
    return jnp.concatenate([jnp.concatenate([a, b], axis=1), jnp.concatenate([b.T, d], axis=1)], axis=0)


def first_kernel(place_ref, half_ref, start_ref, end_ref, out_ref, *turning):
    row = lax.broadcasted_iota(jnp.int32, (128, 128), 0)
    col = lax.broadcasted_iota(jnp.int32, (128, 128), 1)
    packed = half_ref[:128, :]
    mirrored = packed.T
    one = jnp.where(row <= col, packed, mirrored)
    other = jnp.where(row > col, packed, jnp.where(row == col, half_ref[512:513, :], mirrored))
    turn(square(one, half_ref[128:256, :], other), start_ref[0], *turning)
    own_pair = place_ref[0] % 2
    end = end_ref[0, pl.ds(pl.multiple_of(128 * own_pair, 128), 128), :]
    both = pick(end, placed(turning[0], range(4)))
    out_ref[:128, :] = both[:, :128]
    out_ref[128:256, :] = both[:, 128:256]
    out_ref[256:384, :] = dot(both[:, :256], both[:, 256:], NT)
    out_ref[384:, :] = half_ref[256:512, :]


def first_turns(place, half, start, end):
    return pl.pallas_call(
        first_kernel,
        out_shape=jax.ShapeDtypeStruct((640, 128), jnp.float32),
        in_specs=[SMEM, VMEM, VMEM, VMEM],
        out_specs=VMEM,
        scratch_shapes=TURNING,
        compiler_params=LIMIT,
    )(place, half, start, end)


def second_kernel(
    place_ref, own_ref, other_ref, start_ref, end_ref, blocks_ref, matrix_ref, ref1, ref2, ref3, out_ref, rms_ref,
    g_ref, q_ref, matrix_rows, held_rows, squares, in_sems, out_sems, *turning,
):
    x = place_ref[0]
    fetch = [pltpu.make_async_copy(matrix_ref, matrix_rows, in_sems.at[0])]
    for i, ref in enumerate((ref1, ref2, ref3)):
        fetch.append(pltpu.make_async_copy(ref, held_rows.at[i], in_sems.at[i + 1]))
    for copy in fetch:
        copy.start()
    core = place_ref[1]
    g_ref[core] = own_ref[...]
    g_ref[1 - core] = other_ref[...]
    basis = [jnp.concatenate([g_ref[i, :128, :], g_ref[i, 128:256, :]], axis=1) for i in range(2)]
    between = jnp.concatenate(
        [jnp.concatenate([g_ref[i, 384:512, :], g_ref[i, 512:640, :]], axis=1) for i in range(2)], axis=0
    )
    cross = dot(dot(basis[0], between), basis[1], NT)
    turn(square(g_ref[0, 256:384, :], cross, g_ref[1, 256:384, :]), start_ref[1], *turning)
    own_side = place_ref[0] // 2
    end = end_ref[1, pl.ds(pl.multiple_of(128 * own_side, 128), 128), :]
    last = pick(end, placed(turning[0], range(2)))
    turns = jnp.concatenate([dot(last[:, :128], basis[0]), dot(last[:, 128:], basis[1])], axis=1)
    turn_high, turn_low = split(turns, 2)
    for block in range(4):
        cols = slice(128 * block, 128 * block + 128)
        q_ref[block] = jnp.concatenate([turn_high[:, cols], turn_low[:, cols]], axis=0)
    both = jnp.concatenate([q_ref[lax.rem(place_ref[0] + i, 4)] for i in range(4)], axis=1)
    turn_high = both[:128]
    for copy in fetch:
        copy.wait()
    store = []
    for j in range(4):
        rows = pl.ds(pl.multiple_of(QUARTER * lax.rem(x + j, 4), QUARTER), QUARTER)
        parts = [matrix_rows[rows, :]]
        for i in range(1, 4):
            if j == 0:
                parts.append(blocks_ref[lax.rem(x + i, 4)])
            else:
                parts.append(held_rows[i - 1, QUARTER * (j - 1) : QUARTER * j, :])
        high, low = split(jnp.concatenate(parts, axis=1), 2)
        wide = short_dot(high, both, NT)
        value = wide[:, :128] + (wide[:, 128:] + short_dot(low, turn_high, NT))
        squares[j] = value * value
        store.append(pltpu.make_async_copy(squares.at[j], out_ref.at[rows, :], out_sems.at[j]))
        store[-1].start()
    diag = jnp.concatenate([turning[2][0], turning[2][1]], axis=0)
    sums = sum(short_dot(part[:, :8], end, (((0,), (1,)), ((), ()))) for part in reversed(split(diag, 3)))
    rms_ref[...] = jnp.sqrt(jnp.maximum(sums[:1], 0.0) / ROWS + EPS)
    for copy in store:
        copy.wait()


def second_turns(place, own, other, start, end, blocks, matrix, *others):
    rows = matrix.shape[0]
    return pl.pallas_call(
        second_kernel,
        out_shape=(
            jax.ShapeDtypeStruct((rows, 128), jnp.float32),
            jax.ShapeDtypeStruct((1, 128), jnp.float32),
        ),
        in_specs=[SMEM, VMEM, VMEM, VMEM, VMEM, VMEM, HBM, HBM, HBM, HBM],
        out_specs=[HBM, VMEM],
        scratch_shapes=[
            pltpu.VMEM((2, 640, 128), jnp.float32),
            pltpu.VMEM((4, 256, 128), jnp.bfloat16),
            pltpu.VMEM((rows, 128), jnp.float32),
            pltpu.VMEM((3, 3 * QUARTER, 128), jnp.float32),
            pltpu.VMEM((4, QUARTER, 128), jnp.float32),
            pltpu.SemaphoreType.DMA((4,)),
            pltpu.SemaphoreType.DMA((4,)),
            *TURNING,
        ],
        compiler_params=pltpu.CompilerParams(vmem_limit_bytes=52 * 1024 * 1024),
    )(place, own, other, start, end, blocks, matrix, *others)


def other_quarters_kernel(place_ref, m_ref, *refs):
    outs, sems = refs[:3], refs[3]
    copies = []
    for i, out in enumerate(outs):
        for j in range(3):
            quarter = lax.rem(place_ref[0] + 4 - i + j, 4)
            rows = pl.ds(pl.multiple_of(QUARTER * quarter, QUARTER), QUARTER)
            copies.append(pltpu.make_async_copy(m_ref.at[rows, :], out.at[pl.ds(QUARTER * j, QUARTER), :], sems.at[i, j]))
    for copy in copies:
        copy.start()
    for copy in copies:
        copy.wait()


def other_quarters(place, matrix):
    return pl.pallas_call(
        other_quarters_kernel,
        out_shape=(jax.ShapeDtypeStruct((3 * QUARTER, 128), jnp.float32),) * 3,
        in_specs=[SMEM, HBM],
        out_specs=[HBM] * 3,
        scratch_shapes=[pltpu.SemaphoreType.DMA((3, 3))],
        compiler_params=LIMIT,
    )(place, matrix)


def places(order):
    return pl.pallas_call(
        places_kernel,
        out_shape=(jax.ShapeDtypeStruct((2, 256, 256), jnp.bfloat16),) * 2,
        in_specs=[VMEM],
        out_specs=[VMEM, VMEM],
        compiler_params=LIMIT,
    )(order)


def gram_kernel(core_ref, m_ref, mine_ref, theirs_ref):
    parts = [split(jnp.concatenate([m_ref[2 * a], m_ref[2 * a + 1]], axis=1), 2) for a in range(2)]

    def product(left, right):
        (lh, ll), (rh, rl) = left, right
        small = (short_dot(lh, rl, TN) + short_dot(ll, rh, TN)) + short_dot(ll, rl, TN)
        return short_dot(lh, rh, TN) + small

    low, high = slice(0, 128), slice(128, 256)
    between = product(*parts)
    row = lax.broadcasted_iota(jnp.int32, (128, 128), 0)
    col = lax.broadcasted_iota(jnp.int32, (128, 128), 1)
    halves = []
    for i, part in enumerate(parts):
        whole = product(part, part)
        own = (low, high)[i]
        diag = jnp.sum(jnp.where(row == col, whole[high, high], 0.0), axis=0, keepdims=True)
        packed = jnp.where(row <= col, whole[low, low], whole[high, high])
        blocks = [packed, whole[low, high], between[own, low], between[own, high]]
        rest = jnp.zeros((HALF_ROWS - 520, 128), jnp.float32)
        halves.append([*blocks, jnp.broadcast_to(diag, (8, 128)), rest])
    for core in range(2):

        @pl.when(core_ref[0] == core)
        def _(core=core):
            for ref, half in ((mine_ref, halves[core]), (theirs_ref, halves[1 - core])):
                at = 0
                for block in half:
                    ref[at : at + block.shape[0], :] = block
                    at += block.shape[0]


def grams(core_index, blocks):
    return pl.pallas_call(
        gram_kernel,
        out_shape=(jax.ShapeDtypeStruct((HALF_ROWS, 128), jnp.float32),) * 2,
        in_specs=[SMEM, VMEM],
        out_specs=[VMEM, VMEM],
        compiler_params=LIMIT,
    )(core_index, blocks)


def exchange(parts, axes):
    return lax.all_to_all(parts, axes, 0, 0, tiled=True)


def sum_part(value, axes):
    count = lax.axis_size(axes)
    return exchange(value.reshape(count, 1, value.size // count), axes).sum(0)


def collect(value, axes):
    return exchange(jnp.broadcast_to(value[None], (lax.axis_size(axes), *value.shape)), axes)


def swap_cores(value):
    return lax.ppermute(value, "core", ((0, 1), (1, 0)))


def from_next(value, distance):
    return lax.ppermute(value, "x", [((i + distance) % 4, i) for i in range(4)])


def local(matrix, order):
    place = jnp.stack([lax.axis_index("x"), lax.axis_index("core")]).astype(jnp.int32)
    parts = other_quarters(place, matrix)
    blocks = exchange(matrix.reshape(4, QUARTER, 128), "x")
    blocks, *parts = lax.optimization_barrier((blocks, *parts))
    mine, theirs = grams(place[1:], blocks)
    theirs, place, start, end = lax.optimization_barrier((swap_cores(theirs), place, *places(order)))
    gram, *parts = lax.optimization_barrier((mine + theirs, *parts))
    others = [from_next(part, i + 1) for i, part in enumerate(parts)]
    gram = sum_part(gram, ("y", "x"))
    gram = collect(gram, "z").sum(0)
    half = collect(gram, ("y", "x")).reshape(HALF_ROWS, 128)
    half, *others = lax.optimization_barrier((half, *others))
    own = first_turns(place, half, start, end)
    density, rms = second_turns(place, own, swap_cores(own), start, end, blocks, matrix, *others)
    return density, rms.reshape(128)


def solution(mesh):
    fine = Mesh(mesh.devices.reshape(8, 8, 2, 4), ("z", "y", "core", "x"))
    rows = ("z", "y", "core")
    return jax.shard_map(
        local,
        mesh=fine,
        in_specs=(P(rows, "x"), P()),
        out_specs=(P(rows, "x"), P("x")),
        check_vma=False,
    )
```

```python
import jax
import jax.numpy as jnp
from jax import lax
from jax.experimental import pallas as pl
from jax.experimental.pallas import tpu as pltpu
from jax.sharding import Mesh, PartitionSpec as P

ROUNDS = 16
ROWS = 262144
EPS = 1e-06
HIGHEST = lax.Precision.HIGHEST
NN = (((1,), (0,)), ((), ()))
NT = (((1,), (1,)), ((), ()))
TN = (((0,), (0,)), ((), ()))
HALF_ROWS = 544
LIMIT = pltpu.CompilerParams(vmem_limit_bytes=48 * 1024 * 1024)
VMEM = pl.BlockSpec(memory_space=pltpu.VMEM)
SMEM = pl.BlockSpec(memory_space=pltpu.SMEM)
HBM = pl.BlockSpec(memory_space=pltpu.HBM)
QUARTER = 512


def dot(a, b, dims=NN):
    return lax.dot_general(a, b, dims, precision=HIGHEST, preferred_element_type=jnp.float32)


def short_dot(a, b, dims=NN):
    return lax.dot_general(a, b, dims, preferred_element_type=jnp.float32)


def split(value, count):
    parts = []
    for _ in range(count):
        part = value.astype(jnp.bfloat16)
        value = value - part.astype(jnp.float32)
        parts.append(part)
    return parts


def pick(onehot, value, dims=NN):
    high, mid, low = (short_dot(onehot, part, dims) for part in split(value, 3))
    return high + (mid + low)


def slot_at(place, turn):
    side, inner = place // 128, place % 128
    k = 16 * (inner % 8) + inner // 8
    moved = jnp.where(side == 0, turn + k, turn + 255 - k)
    moved = jnp.where(moved >= 255, moved - 255, moved)
    return jnp.where((side == 0) & (k == 0), 255, moved)


def places_kernel(order_ref, start_ref, end_ref):
    rows = lax.broadcasted_iota(jnp.int32, (256, 256), 0)
    cols = lax.broadcasted_iota(jnp.int32, (256, 256), 1)
    first = (slot_at(rows, 0) == cols).astype(jnp.bfloat16)
    last = (slot_at(rows, ROUNDS) == cols).astype(jnp.bfloat16)
    for step in range(2):
        column_slot = (rows == order_ref[step : step + 1, :]).astype(jnp.bfloat16)
        start_ref[step] = short_dot(first, column_slot, NT).astype(jnp.bfloat16)
        end_ref[step] = short_dot(column_slot, last, NT).astype(jnp.bfloat16)


def rotation(cross, low, high):
    x = high - low
    y = cross + cross
    ax = jnp.abs(x)
    yy = y * y
    hh = x * x + yy + 1e-37
    h = hh * lax.rsqrt(hh)
    w = h + ax
    n = lax.rsqrt(w * w + yy)
    big = w * n
    small = y * n
    gap = h * small * small
    back = x < 0.0
    cs = jnp.where(back, small, big)
    sn = jnp.where(back, big, small)
    return cs, sn, jnp.minimum(low, high) - gap, jnp.maximum(low, high) + gap


def one_round(src, dst, dsrc, ddst, cbuf, sbuf):
    row8 = lax.broadcasted_iota(jnp.int32, (8, 128), 0)
    first, last = row8 == 0, row8 == 7

    def put(tops, bottoms, top, bottom):
        for t in range(15):
            tops[pl.ds(8 * t, 8)] = top[t + 1] if t else jnp.where(first, top[0], top[1])
            bottoms[pl.ds(8 * t + 8, 8)] = bottom[t]
        tops[pl.ds(120, 8)] = jnp.where(last, bottom[15], pltpu.roll(top[0], 7, 0))
        bottoms[pl.ds(0, 8)] = jnp.where(first, top[1], pltpu.roll(bottom[15], 1, 0))

    top, bottom = [], []
    for t in range(16):
        rows = pl.ds(8 * t, 8)
        part = src[0, 0, rows] * src[1, 2, rows] + src[0, 1, rows] * src[1, 3, rows]
        cross = jnp.broadcast_to(jnp.sum(part, axis=1, keepdims=True), (8, 128))
        cs, sn, low, high = rotation(cross, dsrc[0, rows], dsrc[1, rows])
        cbuf[rows] = cs
        sbuf[rows] = sn
        top.append(low)
        bottom.append(high)
    put(ddst.at[0], ddst.at[1], top, bottom)
    for lane in range(4):
        top, bottom = [], []
        for t in range(16):
            rows = pl.ds(8 * t, 8)
            cs, sn = cbuf[rows], sbuf[rows]
            p, q = src[0, lane, rows], src[1, lane, rows]
            top.append(cs * p - sn * q)
            bottom.append(sn * p + cs * q)
        put(dst.at[0, lane], dst.at[1, lane], top, bottom)


TURNING = [
    pltpu.VMEM((2, 4, 128, 128), jnp.float32),
    pltpu.VMEM((2, 4, 128, 128), jnp.float32),
    pltpu.VMEM((2, 128, 128), jnp.float32),
    pltpu.VMEM((2, 128, 128), jnp.float32),
    pltpu.VMEM((128, 128), jnp.float32),
    pltpu.VMEM((128, 128), jnp.float32),
]


def turn(gram, start, xa, xb, da, db, cbuf, sbuf):
    start32 = start.astype(jnp.float32)
    held = pick(start, gram)
    diag = jnp.broadcast_to(jnp.sum(start32 * held, axis=1, keepdims=True), (256, 128))
    for side in range(2):
        rows = slice(128 * side, 128 * side + 128)
        da[side] = diag[rows]
        for lane in range(2):
            cols = slice(128 * lane, 128 * lane + 128)
            xa[side, lane] = start32[rows, cols]
            xa[side, lane + 2] = held[rows, cols]

    def two_rounds(_, carry):
        one_round(xa, xb, da, db, cbuf, sbuf)
        one_round(xb, xa, db, da, cbuf, sbuf)
        return carry

    lax.fori_loop(0, ROUNDS // 2, two_rounds, 0, unroll=True)


def placed(xa, lanes):
    sides = [jnp.concatenate([xa[side, lane] for lane in lanes], axis=1) for side in range(2)]
    return jnp.concatenate(sides, axis=0)


def square(a, b, d):
    return jnp.concatenate([jnp.concatenate([a, b], axis=1), jnp.concatenate([b.T, d], axis=1)], axis=0)


def first_kernel(place_ref, half_ref, start_ref, end_ref, out_ref, *turning):
    row = lax.broadcasted_iota(jnp.int32, (128, 128), 0)
    col = lax.broadcasted_iota(jnp.int32, (128, 128), 1)
    packed = half_ref[:128, :]
    mirrored = packed.T
    one = jnp.where(row <= col, packed, mirrored)
    other = jnp.where(row > col, packed, jnp.where(row == col, half_ref[512:513, :], mirrored))
    turn(square(one, half_ref[128:256, :], other), start_ref[0], *turning)
    own_pair = place_ref[0] % 2
    end = end_ref[0, pl.ds(pl.multiple_of(128 * own_pair, 128), 128), :]
    both = pick(end, placed(turning[0], range(4)))
    out_ref[:128, :] = both[:, :128]
    out_ref[128:256, :] = both[:, 128:256]
    out_ref[256:384, :] = dot(both[:, :256], both[:, 256:], NT)
    out_ref[384:, :] = half_ref[256:512, :]


def first_turns(place, half, start, end):
    return pl.pallas_call(
        first_kernel,
        out_shape=jax.ShapeDtypeStruct((640, 128), jnp.float32),
        in_specs=[SMEM, VMEM, VMEM, VMEM],
        out_specs=VMEM,
        scratch_shapes=TURNING,
        compiler_params=LIMIT,
    )(place, half, start, end)


def second_kernel(
    place_ref, own_ref, other_ref, start_ref, end_ref, blocks_ref, matrix_ref, ref1, ref2, ref3, out_ref, rms_ref,
    g_ref, q_ref, matrix_rows, held_rows, squares, in_sems, out_sems, *turning,
):
    x = place_ref[0]
    fetch = [pltpu.make_async_copy(matrix_ref, matrix_rows, in_sems.at[0])]
    for i, ref in enumerate((ref1, ref2, ref3)):
        fetch.append(pltpu.make_async_copy(ref, held_rows.at[i], in_sems.at[i + 1]))
    for copy in fetch:
        copy.start()
    core = place_ref[1]
    g_ref[core] = own_ref[...]
    g_ref[1 - core] = other_ref[...]
    basis = [jnp.concatenate([g_ref[i, :128, :], g_ref[i, 128:256, :]], axis=1) for i in range(2)]
    between = jnp.concatenate(
        [jnp.concatenate([g_ref[i, 384:512, :], g_ref[i, 512:640, :]], axis=1) for i in range(2)], axis=0
    )
    cross = dot(dot(basis[0], between), basis[1], NT)
    turn(square(g_ref[0, 256:384, :], cross, g_ref[1, 256:384, :]), start_ref[1], *turning)
    own_side = place_ref[0] // 2
    end = end_ref[1, pl.ds(pl.multiple_of(128 * own_side, 128), 128), :]
    last = pick(end, placed(turning[0], range(2)))
    turns = jnp.concatenate([dot(last[:, :128], basis[0]), dot(last[:, 128:], basis[1])], axis=1)
    turn_high, turn_low = split(turns, 2)
    for block in range(4):
        cols = slice(128 * block, 128 * block + 128)
        q_ref[block] = jnp.concatenate([turn_high[:, cols], turn_low[:, cols]], axis=0)
    both = jnp.concatenate([q_ref[lax.rem(place_ref[0] + i, 4)] for i in range(4)], axis=1)
    turn_high = both[:128]
    for copy in fetch:
        copy.wait()
    store = []
    for j in range(4):
        rows = pl.ds(pl.multiple_of(QUARTER * lax.rem(x + j, 4), QUARTER), QUARTER)
        parts = [matrix_rows[rows, :]]
        for i in range(1, 4):
            if j == 0:
                parts.append(blocks_ref[lax.rem(x + i, 4)])
            else:
                parts.append(held_rows[i - 1, QUARTER * (j - 1) : QUARTER * j, :])
        high, low = split(jnp.concatenate(parts, axis=1), 2)
        wide = short_dot(high, both, NT)
        value = wide[:, :128] + (wide[:, 128:] + short_dot(low, turn_high, NT))
        squares[j] = value * value
        store.append(pltpu.make_async_copy(squares.at[j], out_ref.at[rows, :], out_sems.at[j]))
        store[-1].start()
    diag = jnp.concatenate([turning[2][0], turning[2][1]], axis=0)
    sums = sum(short_dot(part[:, :8], end, (((0,), (1,)), ((), ()))) for part in reversed(split(diag, 3)))
    rms_ref[...] = jnp.sqrt(jnp.maximum(sums[:1], 0.0) / ROWS + EPS)
    for copy in store:
        copy.wait()


def second_turns(place, own, other, start, end, blocks, matrix, *others):
    rows = matrix.shape[0]
    return pl.pallas_call(
        second_kernel,
        out_shape=(
            jax.ShapeDtypeStruct((rows, 128), jnp.float32),
            jax.ShapeDtypeStruct((1, 128), jnp.float32),
        ),
        in_specs=[SMEM, VMEM, VMEM, VMEM, VMEM, VMEM, HBM, HBM, HBM, HBM],
        out_specs=[HBM, VMEM],
        scratch_shapes=[
            pltpu.VMEM((2, 640, 128), jnp.float32),
            pltpu.VMEM((4, 256, 128), jnp.bfloat16),
            pltpu.VMEM((rows, 128), jnp.float32),
            pltpu.VMEM((3, 3 * QUARTER, 128), jnp.float32),
            pltpu.VMEM((4, QUARTER, 128), jnp.float32),
            pltpu.SemaphoreType.DMA((4,)),
            pltpu.SemaphoreType.DMA((4,)),
            *TURNING,
        ],
        compiler_params=pltpu.CompilerParams(vmem_limit_bytes=52 * 1024 * 1024),
    )(place, own, other, start, end, blocks, matrix, *others)


def other_quarters_kernel(place_ref, m_ref, *refs):
    outs, sems = refs[:3], refs[3]
    copies = []
    for i, out in enumerate(outs):
        for j in range(3):
            quarter = lax.rem(place_ref[0] + 4 - i + j, 4)
            rows = pl.ds(pl.multiple_of(QUARTER * quarter, QUARTER), QUARTER)
            copies.append(pltpu.make_async_copy(m_ref.at[rows, :], out.at[pl.ds(QUARTER * j, QUARTER), :], sems.at[i, j]))
    for copy in copies:
        copy.start()
    for copy in copies:
        copy.wait()


def other_quarters(place, matrix):
    return pl.pallas_call(
        other_quarters_kernel,
        out_shape=(jax.ShapeDtypeStruct((3 * QUARTER, 128), jnp.float32),) * 3,
        in_specs=[SMEM, HBM],
        out_specs=[HBM] * 3,
        scratch_shapes=[pltpu.SemaphoreType.DMA((3, 3))],
        compiler_params=LIMIT,
    )(place, matrix)


def places(order):
    return pl.pallas_call(
        places_kernel,
        out_shape=(jax.ShapeDtypeStruct((2, 256, 256), jnp.bfloat16),) * 2,
        in_specs=[VMEM],
        out_specs=[VMEM, VMEM],
        compiler_params=LIMIT,
    )(order)


def gram_kernel(core_ref, m_ref, mine_ref, theirs_ref):
    parts = [split(jnp.concatenate([m_ref[2 * a], m_ref[2 * a + 1]], axis=1), 2) for a in range(2)]

    def product(left, right):
        (lh, ll), (rh, rl) = left, right
        small = (short_dot(lh, rl, TN) + short_dot(ll, rh, TN)) + short_dot(ll, rl, TN)
        return short_dot(lh, rh, TN) + small

    low, high = slice(0, 128), slice(128, 256)
    between = product(*parts)
    row = lax.broadcasted_iota(jnp.int32, (128, 128), 0)
    col = lax.broadcasted_iota(jnp.int32, (128, 128), 1)
    halves = []
    for i, part in enumerate(parts):
        whole = product(part, part)
        own = (low, high)[i]
        diag = jnp.sum(jnp.where(row == col, whole[high, high], 0.0), axis=0, keepdims=True)
        packed = jnp.where(row <= col, whole[low, low], whole[high, high])
        blocks = [packed, whole[low, high], between[own, low], between[own, high]]
        rest = jnp.zeros((HALF_ROWS - 520, 128), jnp.float32)
        halves.append([*blocks, jnp.broadcast_to(diag, (8, 128)), rest])
    for core in range(2):

        @pl.when(core_ref[0] == core)
        def _(core=core):
            for ref, half in ((mine_ref, halves[core]), (theirs_ref, halves[1 - core])):
                at = 0
                for block in half:
                    ref[at : at + block.shape[0], :] = block
                    at += block.shape[0]


def grams(core_index, blocks):
    return pl.pallas_call(
        gram_kernel,
        out_shape=(jax.ShapeDtypeStruct((HALF_ROWS, 128), jnp.float32),) * 2,
        in_specs=[SMEM, VMEM],
        out_specs=[VMEM, VMEM],
        compiler_params=LIMIT,
    )(core_index, blocks)


def exchange(parts, axes):
    return lax.all_to_all(parts, axes, 0, 0, tiled=True)


def sum_part(value, axes):
    count = lax.axis_size(axes)
    return exchange(value.reshape(count, 1, value.size // count), axes).sum(0)


def collect(value, axes):
    return exchange(jnp.broadcast_to(value[None], (lax.axis_size(axes), *value.shape)), axes)


def swap_cores(value):
    return lax.ppermute(value, "core", ((0, 1), (1, 0)))


def from_next(value, distance):
    return lax.ppermute(value, "x", [((i + distance) % 4, i) for i in range(4)])


def local(matrix, order):
    place = jnp.stack([lax.axis_index("x"), lax.axis_index("core")]).astype(jnp.int32)
    parts = other_quarters(place, matrix)
    blocks = exchange(matrix.reshape(4, QUARTER, 128), "x")
    blocks, *parts = lax.optimization_barrier((blocks, *parts))
    mine, theirs = grams(place[1:], blocks)
    theirs, place, start, end = lax.optimization_barrier((swap_cores(theirs), place, *places(order)))
    gram, *parts = lax.optimization_barrier((mine + theirs, *parts))
    others = [from_next(part, i + 1) for i, part in enumerate(parts)]
    gram = sum_part(gram, ("y", "x"))
    gram = collect(gram, "z").sum(0)
    half = collect(gram, ("y", "x")).reshape(HALF_ROWS, 128)
    own = first_turns(place, half, start, end)
    own, *others = lax.optimization_barrier((own, *others))
    density, rms = second_turns(place, own, swap_cores(own), start, end, blocks, matrix, *others)
    return density, rms.reshape(128)


def solution(mesh):
    fine = Mesh(mesh.devices.reshape(8, 8, 2, 4), ("z", "y", "core", "x"))
    rows = ("z", "y", "core")
    return jax.shard_map(
        local,
        mesh=fine,
        in_specs=(P(rows, "x"), P()),
        out_specs=(P(rows, "x"), P("x")),
        check_vma=False,
    )
```
